128 devices in a mesh: shard: 2 (over x_hi), ctx: 16 (over x_lo, z, core), tp: 4 (over y).
Axes of the slice: x: 4 (x_hi: 2, x_lo: 2; x = x_hi * 2 + x_lo), y: 4, z: 4, core: 2. Of those that a mesh axis runs over, the one named last changes fastest.
Arguments:
- block_input: bfloat16 [4, 4096, 1024], P('shard', 'ctx', 'tp'), may hold values from -6 to 6
- in_proj: bfloat16 [1024, 3, 1024], P('shard', None, 'tp'), may hold values from -0.1875 to 0.1875
- out_proj: bfloat16 [1024, 1024], P('tp', 'shard'), may hold values from -0.1875 to 0.1875
- gate_proj: bfloat16 [1024, 4608], P('shard', 'tp'), may hold values from -0.1875 to 0.1875
- up_proj: bfloat16 [1024, 4608], P('shard', 'tp'), may hold values from -0.1875 to 0.1875
- down_proj: bfloat16 [4608, 1024], P('tp', 'shard'), may hold values from -0.09375 to 0.09375
- mixer_gain: float32 [1024], P('tp'), may hold values from 0.5 to 1.5
- ffn_gain: float32 [1024], P('tp'), may hold values from 0.5 to 1.5
- conv_kernel: float32 [3, 1024], P(None, 'tp'), may hold values from -3.5 to 3.5
- cotangent: bfloat16 [4, 4096, 1024], P('shard', 'ctx', 'tp'), may hold values from -6 to 6
Outputs:
- block_out: bfloat16 [4, 4096, 1024], P('shard', 'ctx', 'tp')
- input_grad: float32 [4, 4096, 1024], P('shard', 'ctx', 'tp')
- in_proj_grad: float32 [1024, 3, 1024], P(('shard', 'ctx'), None, 'tp')
- out_proj_grad: float32 [1024, 1024], P('tp', ('shard', 'ctx'))
- gate_grad: float32 [1024, 4608], P(('shard', 'ctx'), 'tp')
- up_grad: float32 [1024, 4608], P(('shard', 'ctx'), 'tp')
- down_grad: float32 [4608, 1024], P('tp', ('shard', 'ctx'))
- mixer_gain_grad: float32 [1024], P('tp')
- ffn_gain_grad: float32 [1024], P('tp')
- kernel_grad: float32 [3, 1024], P(None, 'tp')
The draws below stay inside these ranges and needn't reach their ends.
All inputs are finite; a program needn't handle non-finite values.
Results may differ from the reference program's by a relative error of at most 0.0088.
Values may be sent and summed in bfloat16 or wider, within the bound.
A program may use at most 128 MiB of HBM per device.

```python
import jax
import jax.numpy as jnp
from jax import lax

D = 1024
FF = 4608
KW = 3
LENGTH = 4096
SEQS = 4


def strengthened(drawn, own_key, source, target, blocks, factor):
    def block_of(axis_at):
        return (jnp.arange(drawn.shape[axis_at]) // (drawn.shape[axis_at] // blocks)).reshape((-1,) + (1,) * (drawn.ndim - 1 - axis_at))

    one_side = jax.random.permutation(own_key, blocks)[block_of(target)]
    other_side = (block_of(target) + blocks // 2) % blocks
    return jnp.where((block_of(source) == one_side) | (block_of(source) == other_side), factor * drawn, drawn)


def shard_levels(rng, extent, split, smallest, largest):
    loudness, own = 1.0, jax.random.fold_in(rng, 6)
    for dim, shards_of in split:
        heights = jnp.exp(jax.random.uniform(jax.random.fold_in(own, dim), (shards_of,), jnp.float32, smallest / len(split), largest / len(split)))
        loudness = loudness * jnp.repeat(heights, extent[dim] // shards_of).reshape([-1 if axis == dim else 1 for axis in range(len(extent))])
    return loudness


def centred(stream_key, dims, scale, bound, cuts=(), held_as=jnp.bfloat16):
    level = shard_levels(stream_key, dims, cuts, -0.22, 0.18) if cuts else 1.0
    drawn = jax.random.normal(stream_key, dims, jnp.float32) * scale * level
    return jnp.minimum(jnp.maximum(drawn, -bound), bound).astype(held_as)


def heavy_noise(key, extent, deviation, reach, shards, heavy, held_as=jnp.bfloat16):
    values = deviation * jax.random.normal(key, extent, jnp.float32)
    if shards:
        values = values * shard_levels(key, extent, shards, -0.22, 0.18)
    return jnp.clip(strengthened(values, jax.random.fold_in(key, 3), *heavy), -reach, reach).astype(held_as)


def setup_inputs(seed: int = 0) -> dict:
    keys = jax.random.split(jax.random.key(seed), 11)
    block_input = heavy_noise(keys[0], (SEQS, LENGTH, D), 1.0, 6.0, ((0, 2), (1, 16), (2, 4)), (1, 2, 16, 2.0))
    in_proj = centred(keys[1], (D, 3, D), D ** -0.5, 0.1875, ((0, 2), (2, 4)))
    out_proj = centred(keys[2], (D, D), D ** -0.5, 0.1875, ((0, 4), (1, 2)))
    gate_proj = centred(keys[3], (D, FF), D ** -0.5, 0.1875, ((0, 2), (1, 4)))
    up_proj = centred(keys[4], (D, FF), D ** -0.5, 0.1875, ((0, 2), (1, 4)))
    down_proj = centred(keys[5], (FF, D), FF ** -0.5, 0.09375, ((0, 4), (1, 2)))
    mixer_gain = jnp.clip(1.0 + 0.1 * jax.random.normal(keys[6], (D,), jnp.float32), 0.5, 1.5)
    ffn_gain = jnp.clip(1.0 + 0.1 * jax.random.normal(keys[7], (D,), jnp.float32), 0.5, 1.5)
    conv_kernel = centred(keys[8], (KW, D), KW ** -0.5, 3.5, ((1, 4),), jnp.float32)
    cotangent = heavy_noise(keys[9], (SEQS, LENGTH, D), 1.0, 6.0, ((0, 2), (1, 16), (2, 4)), (1, 2, 16, 2.0))
    return {"block_input": block_input, "in_proj": in_proj, "out_proj": out_proj, "gate_proj": gate_proj, "up_proj": up_proj, "down_proj": down_proj, "mixer_gain": mixer_gain, "ffn_gain": ffn_gain, "conv_kernel": conv_kernel, "cotangent": cotangent}


EPS = 1e-05

@jax.custom_vjp
def low(v):
    return lax.optimization_barrier(v.astype(jnp.bfloat16)).astype(jnp.float32)

@jax.custom_vjp
def lower_backward(v):
    return v

def low_keep(v):
    return (low(v), None)

def low_pass(kept, grad):
    return (grad,)

def back_keep(v):
    return (v, None)

def back_low(kept, grad):
    return (low(grad),)
low.defvjp(low_keep, low_pass)
lower_backward.defvjp(back_keep, back_low)

def norm_rows(values, norm_gain):
    return values * lax.rsqrt(lax.optimization_barrier(jnp.mean(values * values, axis=-1, keepdims=True)) + EPS) * norm_gain

def forward(inputs, input_weight, output_weight, gate_weight, up_weight, down_weight, mixer_gain, ffn_gain, conv_kernel):
    highest_precision = lax.Precision.HIGHEST
    first_normalized = low(norm_rows(inputs, mixer_gain))
    projected_rows = lower_backward(jnp.einsum('iqa,ayj->iqyj', first_normalized, input_weight, precision=highest_precision))
    b_gate = projected_rows[:, :, 0]
    c_gate = projected_rows[:, :, 1]
    x_in = projected_rows[:, :, 2]
    mixed = low(b_gate * x_in)
    padded = jnp.pad(mixed, ((0, 0), (2, 0), (0, 0)))
    convolved = conv_kernel[0] * padded[:, :-2] + conv_kernel[1] * padded[:, 1:-1] + conv_kernel[2] * padded[:, 2:]
    gated_product = low(c_gate * convolved)
    branch_output = lower_backward(jnp.einsum('ynz,zj->ynj', gated_product, output_weight, precision=highest_precision))
    residual_state = inputs + branch_output
    second_normalized = low(norm_rows(residual_state, ffn_gain))
    gate_activation = lower_backward(jnp.einsum('zxw,wt->zxt', second_normalized, gate_weight, precision=highest_precision))
    up_activation = lower_backward(jnp.einsum('zxw,wt->zxt', second_normalized, up_weight, precision=highest_precision))
    hidden_state = low(jax.nn.silu(gate_activation) * up_activation)
    return residual_state + jnp.einsum('hcu,uv->hcv', hidden_state, down_weight, precision=highest_precision)

def reference(block_input, in_proj, out_proj, gate_proj, up_proj, down_proj, mixer_gain, ffn_gain, conv_kernel, cotangent):
    weights = (block_input.astype(jnp.float32), in_proj.astype(jnp.float32), out_proj.astype(jnp.float32), gate_proj.astype(jnp.float32), up_proj.astype(jnp.float32), down_proj.astype(jnp.float32), mixer_gain.astype(jnp.float32), ffn_gain.astype(jnp.float32), conv_kernel.astype(jnp.float32))
    result, pullback = jax.vjp(forward, *weights)
    grads = pullback(cotangent.astype(jnp.float32))
    return (result.astype(jnp.bfloat16), grads[0], grads[1], grads[2], grads[3], grads[4], grads[5], grads[6], grads[7], grads[8])
```

```python
import types

import jax
import jax.numpy as jnp
from jax import lax
from jax.experimental import pallas as pl
from jax.experimental.pallas import tpu as pltpu
from jax.sharding import PartitionSpec as P

EPS = 1e-05
MESH = pl.DeviceIdType.MESH
f32, bf16 = jnp.float32, jnp.bfloat16
WIDE, SEQ, TOK, CH, HID = 1024, 256, 512, 256, 1152
DOWN, GATE, UP, OUT, IN = range(5)
COLS = (HID, HID, HID, CH, 3 * CH)
RIGHT, LEFT, ACROSS, CORE, Z1, X1, Z3, X3, NEXT, PREV = range(10)
AHEAD, GATHER, SUM, TOTAL, GRAD, GAINS, EDGE, BACK, SMALL = range(9)
X, COT, Q, B = range(5, 9)
ORDERS = {
    DOWN: ((Z1, X1, Z3, X3), (Z3, X3, Z1, X1)),
    GATE: ((X1, Z1, X3, Z3), (X3, Z3, X1, Z1)),
    UP: ((Z1, X3, Z3, X1), (X1, Z3, X3, Z1)),
    OUT: ((Z3, X1, Z1, X3), (X3, Z1, X1, Z3)),
    IN: ((Z1, X1, Z3, X3), (X3, Z3, X1, Z1)),
}
OFFSETS = (0, 8, 12, 14)


def scratch():
    v = pltpu.VMEM
    shapes = dict(
        xg=v((TOK, WIDE), bf16),
        cg=v((TOK, WIDE), bf16),
        qg=v((TOK, WIDE), bf16),
        bg=v((TOK, WIDE), bf16),
        n1=v((TOK, WIDE), bf16),
        gains=v((8, WIDE), f32),
        r1=v((TOK, 1), f32),
        r2=v((TOK, 1), f32),
        col=v((2, TOK, 1), f32),
        wi=v((3, WIDE, CH), bf16),
        wo=v((CH, WIDE), bf16),
        wg=v((WIDE, HID), bf16),
        wu=v((WIDE, HID), bf16),
        wd=v((HID, WIDE), bf16),
        proj=v((3, TOK, CH), f32),
        mpad=v((2, SEQ + 8, CH), f32),
        hs=v((2, 16, CH), bf16),
        hr=v((2, 16, CH), bf16),
        conv=v((TOK, CH), f32),
        gated=v((TOK, CH), bf16),
        ys=v((4, 2, 3, SEQ, CH), bf16),
        yr=v((4, 2, 2, SEQ, CH), bf16),
        yo=v((4, 2, 2, SEQ // 2, CH), bf16),
        own=v((4, TOK, CH), f32),
        resid=v((TOK, CH), f32),
        tg=v((SEQ, HID), f32),
        tu=v((SEQ, HID), f32),
        td=v((SEQ, HID), f32),
        lanes=v((SEQ, 128), f32),
        hid=v((TOK, HID), bf16),
        eg=v((TOK, HID), bf16),
        eu=v((TOK, HID), bf16),
        dres=v((TOK, CH), f32),
        dpad=v((2, SEQ + 8, CH), f32),
        ds=v((2, 8, CH), f32),
        dr=v((2, 8, CH), f32),
        dproj=v((TOK, 3 * CH), bf16),
        rso=v((2, 2, 8, SEQ), f32),
        rsr=v((2, 2, 3, 8, SEQ), f32),
        sums=v((6, 8, CH), f32),
        sumr=v((5, 8, CH), f32),
        terms=[v((2, 2, 16, 16, n), bf16) for n in COLS],
        paired=[v((2, 16, 16, n), bf16) for n in COLS],
        came=[v((2, 15, 16, n), bf16) for n in COLS],
        ssem=pltpu.SemaphoreType.DMA((256,)),
        rsem=pltpu.SemaphoreType.DMA((256,)),
        lsem=pltpu.SemaphoreType.DMA((16,)),
    )
    return shapes


def nn(a, b):
    return jnp.dot(a, b, preferred_element_type=f32)


def nt(a, b):
    return lax.dot_general(a, b, (((1,), (1,)), ((), ())), preferred_element_type=f32)


def tn(a, b):
    return lax.dot_general(a, b, (((0,), (0,)), ((), ())), preferred_element_type=f32)


def row_of(lanes):
    ones = jnp.ones((8, lanes.shape[1]), f32)
    return lax.dot_general(
        ones, lanes, (((1,), (1,)), ((), ())), precision=lax.Precision.HIGHEST, preferred_element_type=f32
    )


def block_kernel(r, *refs):
    (x_hbm, cot_hbm, in_hbm, out_hbm, gate_hbm, up_hbm, down_hbm, mg, fg, taps) = refs[:10]
    (block_out, input_grad, g_in, g_out, g_gate, g_up, g_down, g_small) = refs[10:]
    grads = {DOWN: g_down, GATE: g_gate, UP: g_up, OUT: g_out, IN: g_in}
    ssem, rsem, lsem = r.ssem, r.rsem, r.lsem

    shard, ctx, t = lax.axis_index("shard"), lax.axis_index("ctx"), lax.axis_index("tp")
    core, z, x = ctx % 2, (ctx // 2) % 4, shard * 2 + ctx // 8

    def dev(xx, zz, cc, tt):
        return (xx // 2, (xx % 2) * 8 + zz * 2 + cc, tt)

    z1, z3, x1, x3 = z + 1 - 2 * (z % 2), 3 - z, x + 1 - 2 * (x % 2), 3 - x
    right, left, across = (t + 1) % 4, (t + 3) % 4, (t + 2) % 4
    to = {
        RIGHT: (shard, ctx, right),
        LEFT: (shard, ctx, left),
        ACROSS: (shard, ctx, across),
        CORE: dev(x, z, 1 - core, t),
        Z1: dev(x, z1, core, t),
        Z3: dev(x, z3, core, t),
        X1: dev(x1, z, core, t),
        X3: dev(x3, z, core, t),
        NEXT: (shard, (ctx + 1) % 16, t),
        PREV: (shard, (ctx + 15) % 16, t),
    }

    ids, sent, local = {}, [], {}
    gathered = {X: r.xg, COT: r.cg, Q: r.qg, B: r.bg}

    def number(key):
        return ids.setdefault(key, len(ids))

    def send(key, src, dst, where):
        n = number(key)
        copy = pltpu.make_async_remote_copy(
            src_ref=src,
            dst_ref=dst,
            send_sem=ssem.at[n],
            recv_sem=rsem.at[n],
            device_id=to[where],
            device_id_type=MESH,
        )
        copy.start()
        sent.append(copy)

    def arrived(key, dst):
        pltpu.make_async_copy(dst, dst, rsem.at[number(key)]).wait()

    def fetch(key, src, dst):
        copy = pltpu.make_async_copy(src, dst, lsem.at[len(local)])
        copy.start()
        local[key] = copy

    def part(n):
        return pl.ds(pl.multiple_of(n * CH, CH), CH)

    def rows_of(s):
        return pl.ds(s * SEQ, SEQ)

    weights = {
        IN: (in_hbm, r.wi, 512),
        OUT: (out_hbm, r.wo, 256),
        GATE: (gate_hbm, r.wg, 512),
        UP: (up_hbm, r.wu, 512),
        DOWN: (down_hbm, r.wd, HID),
    }

    def piece(w, half, first, count):
        whole = weights[w][1]
        if w == IN:
            return whole.at[:, pl.ds(pl.multiple_of(half * 512 + first, 32), count), :]
        if w in (GATE, UP):
            return whole.at[pl.ds(pl.multiple_of(half * 512 + first, 32), count), :]
        return whole.at[pl.ds(pl.multiple_of(first, 16), count), pl.ds(pl.multiple_of(half * 512, 512), 512)]

    def source(w, first, count):
        held = weights[w][0]
        at = pl.ds(pl.multiple_of(first, 16), count)
        return held.at[:, at, :] if w == IN else held.at[at, :]

    def quarter(w):
        return weights[w][2] // 4

    pair = z % 2

    def weight_own(w):
        fetch(w, weights[w][0], piece(w, shard, 0, weights[w][2]))

    def weight_cross(w):
        n = quarter(w)
        first = (pair * 2 + core) * n
        send((AHEAD, w, 0), source(w, first, n), piece(w, shard, first, n), X3)

    def weight_around(w):
        n = quarter(w)
        first = (pair * 2 + core) * n
        mine = piece(w, 1 - shard, first, n)
        arrived((AHEAD, w, 0), mine)
        a, b = piece(w, 1 - shard, first, n // 2), piece(w, 1 - shard, first + n // 2, n // 2)
        send((AHEAD, w, 1), a, a, Z1)
        send((AHEAD, w, 2), b, b, Z3)
        send((AHEAD, w, 3), mine, mine, CORE)

    def weight_share(w):
        n = quarter(w)
        first = ((1 - pair) * 2 + core) * n
        arrived((AHEAD, w, 1), piece(w, 1 - shard, first, n // 2))
        arrived((AHEAD, w, 2), piece(w, 1 - shard, first + n // 2, n // 2))
        other = piece(w, 1 - shard, first, n)
        send((AHEAD, w, 4), other, other, CORE)

    def weight_ready(w):
        n = quarter(w)
        arrived((AHEAD, w, 3), piece(w, 1 - shard, (pair * 2 + 1 - core) * n, n))
        arrived((AHEAD, w, 4), piece(w, 1 - shard, ((1 - pair) * 2 + 1 - core) * n, n))
        local[w].wait()

    def gather_start(name, src, s):
        whole = gathered[name]
        dst = whole.at[rows_of(s), part(t)]
        send((GATHER, name, s, 0), src, dst, RIGHT)
        send((GATHER, name, s, 1), src, dst, LEFT)

    def gather_relay(name, s):
        whole = gathered[name]
        arrived((GATHER, name, s, 0), whole.at[rows_of(s), part(left)])
        a = whole.at[pl.ds(s * SEQ, SEQ // 2), part(left)]
        send((GATHER, name, s, 2), a, a, RIGHT)
        arrived((GATHER, name, s, 1), whole.at[rows_of(s), part(right)])
        b = whole.at[pl.ds(s * SEQ + SEQ // 2, SEQ // 2), part(right)]
        send((GATHER, name, s, 3), b, b, LEFT)

    def gather_finish(name, s):
        whole = gathered[name]
        arrived((GATHER, name, s, 2), whole.at[pl.ds(s * SEQ, SEQ // 2), part(across)])
        arrived((GATHER, name, s, 3), whole.at[pl.ds(s * SEQ + SEQ // 2, SEQ // 2), part(across)])

    top, low = pl.ds(0, SEQ // 2), pl.ds(SEQ // 2, SEQ // 2)

    def sum_start(ph, s, block):
        ys, yr, yo = r.ys, r.yr, r.yo
        ys[ph, s, 2] = block(across).astype(bf16)
        send((SUM, ph, s, 0), ys.at[ph, s, 2, top], yo.at[ph, s, 0], RIGHT)
        send((SUM, ph, s, 1), ys.at[ph, s, 2, low], yo.at[ph, s, 1], LEFT)
        ys[ph, s, 0] = block(right).astype(bf16)
        send((SUM, ph, s, 2), ys.at[ph, s, 0, low], yr.at[ph, s, 0, low], RIGHT)
        ys[ph, s, 1] = block(left).astype(bf16)
        send((SUM, ph, s, 3), ys.at[ph, s, 1, top], yr.at[ph, s, 1, top], LEFT)
        r.own[ph, rows_of(s), :] = block(t)

    def sum_relay(ph, s):
        ys, yr, yo = r.ys, r.yr, r.yo
        arrived((SUM, ph, s, 0), yo.at[ph, s, 0])
        ys[ph, s, 0, top, :] = (ys[ph, s, 0, top, :].astype(f32) + yo[ph, s, 0].astype(f32)).astype(bf16)
        send((SUM, ph, s, 4), ys.at[ph, s, 0, top], yr.at[ph, s, 0, top], RIGHT)
        arrived((SUM, ph, s, 1), yo.at[ph, s, 1])
        ys[ph, s, 1, low, :] = (ys[ph, s, 1, low, :].astype(f32) + yo[ph, s, 1].astype(f32)).astype(bf16)
        send((SUM, ph, s, 5), ys.at[ph, s, 1, low], yr.at[ph, s, 1, low], LEFT)

    def sum_finish(ph, s):
        yr = r.yr
        arrived((SUM, ph, s, 2), yr.at[ph, s, 0, low])
        arrived((SUM, ph, s, 3), yr.at[ph, s, 1, top])
        arrived((SUM, ph, s, 4), yr.at[ph, s, 0, top])
        arrived((SUM, ph, s, 5), yr.at[ph, s, 1, low])

    def summed(ph, s, i, n):
        at = pl.ds(i, n)
        own = r.own[ph, pl.ds(s * SEQ + i, n), :]
        return own + r.yr[ph, s, 0, at, :].astype(f32) + r.yr[ph, s, 1, at, :].astype(f32)

    def totals_start(kind, s, lanes):
        r.rso[kind, s] = row_of(lanes)
        for slot, where in enumerate((RIGHT, LEFT, ACROSS)):
            send((TOTAL, kind, s, slot), r.rso.at[kind, s], r.rsr.at[kind, s, slot], where)

    def totals_finish(kind, s):
        total = r.rso[kind, s]
        for slot in range(3):
            arrived((TOTAL, kind, s, slot), r.rsr.at[kind, s, slot])
            total = total + r.rsr[kind, s, slot]
        r.col[kind, rows_of(s), :] = jnp.transpose(total)[:, 0:1]

    def grad_product(g, lhs, rhs):
        held, width = r.terms[g], COLS[g]

        @pl.loop(0, 4)
        def _(xp):
            a = lhs[:, part(xp)]
            hi, lo = (xp // 2 + x // 2) % 2, (xp + x) % 2
            bits = {X3: hi, X1: (lo + hi) % 2}
            for first in range(0, width, 256):
                n = min(256, width - first)
                value = tn(a, rhs[:, first : first + n]).astype(bf16)
                for zp in range(4):
                    zh, zl = (zp // 2 + z // 2) % 2, (zp + z) % 2
                    bits[Z3], bits[Z1] = zh, (zl + zh) % 2
                    for cp in range(2):
                        mine = (cp + core) % 2
                        for half in range(2):
                            pos = 0
                            for d in ORDERS[g][half]:
                                pos = 2 * pos + bits[d]
                            at = (zp * 2 + cp) * 32 + half * 16
                            held[mine, half, pos, :, first : first + n] = value[at : at + 16]

        send((GRAD, g), held.at[1], r.paired[g], CORE)

    def grad_send(g, stage):
        n = 8 >> stage
        for half in range(2):
            send(
                (GRAD, g, half, stage),
                r.terms[g].at[0, half, pl.ds(n, n)],
                r.came[g].at[half, pl.ds(OFFSETS[stage], n)],
                ORDERS[g][half][stage],
            )

    def grad_first(g):
        held, came = r.terms[g], r.paired[g]
        arrived((GRAD, g), came)

        @pl.loop(0, 16)
        def _(i):
            for half in range(2):
                held[0, half, i] = (held[0, half, i].astype(f32) + came[half, i].astype(f32)).astype(bf16)

        grad_send(g, 0)

    def grad_next(g, stage):
        held, came = r.terms[g], r.came[g]
        n = 16 >> stage
        first = OFFSETS[stage - 1]
        for half in range(2):
            arrived((GRAD, g, half, stage - 1), came.at[half, pl.ds(first, n)])

        @pl.loop(0, n)
        def _(i):
            for half in range(2):
                held[0, half, i] = (held[0, half, i].astype(f32) + came[half, first + i].astype(f32)).astype(bf16)

        grad_send(g, stage)

    def grad_last(g):
        held, came = r.terms[g], r.came[g]
        for half in range(2):
            arrived((GRAD, g, half, 3), came.at[half, pl.ds(14, 1)])
            total = held[0, half, 0].astype(f32) + came[half, 14].astype(f32)
            rows = pl.ds(half * 16, 16)
            if g == IN:
                for k in range(3):
                    g_in[k, rows, :] = total[:, k * CH : (k + 1) * CH]
            else:
                grads[g][rows, :] = total

    def in_rows(s, step, body):
        @pl.loop(0, SEQ // step)
        def _(n):
            i = pl.multiple_of(n * step, step)
            body(i, pl.ds(pl.multiple_of(s * SEQ + i, step), step))

    barrier = pltpu.get_barrier_semaphore()
    for where in to:
        pl.semaphore_signal(barrier, inc=1, device_id=to[where], device_id_type=MESH)
    fetch(X, x_hbm, r.xg.at[:, part(t)])
    fetch(COT, cot_hbm, r.cg.at[:, part(t)])
    for w in (IN, OUT, GATE, UP, DOWN):
        weight_own(w)
    own_gains = r.gains.at[:, part(t)]
    own_gains[...] = jnp.zeros((8, CH), f32)
    own_gains[0:1, :] = mg[...]
    own_gains[1:2, :] = fg[...]
    pl.semaphore_wait(barrier, len(to))

    for s in range(2):
        gather_start(X, x_hbm.at[rows_of(s)], s)
    for where in (RIGHT, LEFT, ACROSS):
        send((GAINS, where), own_gains, own_gains, where)
    for w in (IN, OUT, GATE, UP, DOWN):
        weight_cross(w)
    for s in range(2):
        gather_relay(X, s)
    for s in range(2):
        gather_start(COT, cot_hbm.at[rows_of(s)], s)
    weight_around(IN)
    local[X].wait()
    for where, block in ((RIGHT, left), (LEFT, right), (ACROSS, across)):
        arrived((GAINS, where), r.gains.at[:, part(block)])

    def normalise(s):
        def body(i, rows):
            v = r.xg[rows, :].astype(f32)
            scale = lax.rsqrt(jnp.sum(v * v, axis=1, keepdims=True) / WIDE + EPS)
            r.r1[rows, :] = scale
            r.n1[rows, :] = (v * scale * r.gains[0:1, :]).astype(bf16)

        in_rows(s, 32, body)

    def project(s):
        for k in range(3):
            r.proj[k, rows_of(s), :] = nn(r.n1[rows_of(s), :], r.wi[k])
        mixed = (r.proj[0, rows_of(s), :] * r.proj[2, rows_of(s), :]).astype(bf16)
        r.mpad[s, pl.ds(8, SEQ), :] = mixed.astype(f32)
        r.hs[s] = mixed[SEQ - 16 :]
        send((EDGE, s), r.hs.at[s], r.hr.at[s], NEXT)

    gather_finish(X, 0)
    normalise(0)
    gather_finish(X, 1)
    normalise(1)
    weight_share(IN)
    weight_around(OUT)
    weight_around(GATE)
    weight_ready(IN)
    project(0)
    project(1)
    weight_share(OUT)
    for s in range(2):
        gather_relay(COT, s)
    weight_around(UP)

    def branch(s):
        arrived((EDGE, s), r.hr.at[s])
        edge = r.hr[s].astype(f32)[8:16]
        r.mpad[s, 0:8, :] = jnp.where(ctx > 0, edge, 0.0)

        for i in range(0, SEQ, 64):
            rows = pl.ds(s * SEQ + i, 64)
            c = (
                taps[0:1, :] * r.mpad[s, i + 6 : i + 70, :]
                + taps[1:2, :] * r.mpad[s, i + 7 : i + 71, :]
                + taps[2:3, :] * r.mpad[s, i + 8 : i + 72, :]
            )
            r.conv[rows, :] = c
            r.gated[rows, :] = (r.proj[1, rows, :] * c).astype(bf16)

        sum_start(0, s, lambda n: nn(r.gated[rows_of(s), :], r.wo[:, part(n)]))

    weight_ready(OUT)
    branch(0)
    branch(1)
    sum_relay(0, 0)
    weight_share(GATE)
    sum_relay(0, 1)
    weight_around(DOWN)
    weight_share(UP)

    def second(s):
        sum_finish(0, s)

        def body(i, rows):
            value = r.xg[rows, part(t)].astype(f32) + summed(0, s, i, 32)
            r.resid[rows, :] = value
            r.qg[rows, part(t)] = (value * fg[...]).astype(bf16)

        in_rows(s, 32, body)
        gather_start(Q, r.qg.at[rows_of(s), part(t)], s)

    second(0)
    second(1)
    gather_relay(Q, 0)
    gather_relay(Q, 1)
    local[COT].wait()
    weight_share(DOWN)
    gather_finish(COT, 0)
    gather_finish(COT, 1)
    for w in (GATE, UP, DOWN):
        weight_ready(w)

    def feed(s):
        gather_finish(Q, s)

        def scales(i, rows):
            v = r.qg[rows, :].astype(f32) * (1.0 / r.gains[1:2, :])
            r.r2[rows, :] = lax.rsqrt(jnp.sum(v * v, axis=1, keepdims=True) / WIDE + EPS)

        in_rows(s, 32, scales)
        q, c = r.qg[rows_of(s), :], r.cg[rows_of(s), :]
        for first in range(0, HID, 256):
            cols = pl.ds(first, min(256, HID - first))
            r.tg[:, cols] = nn(q, r.wg[:, cols])
            r.tu[:, cols] = nn(q, r.wu[:, cols])
            r.td[:, cols] = nt(c, r.wd[cols, :])

        def body(i, rows):
            here = pl.ds(i, 16)
            scale = r.r2[rows, :]
            total = jnp.zeros((16, 128), f32)
            for first in range(0, HID, 384):
                cols = pl.ds(first, 384)
                gate, up, dh = r.tg[here, cols] * scale, r.tu[here, cols] * scale, r.td[here, cols]
                sg = jax.nn.sigmoid(gate)
                act = gate * sg
                r.hid[rows, cols] = (act * up).astype(bf16)
                d_gate = dh * up * sg * (1.0 + gate * (1.0 - sg))
                d_up = dh * act
                r.eg[rows, cols] = (d_gate * scale).astype(bf16)
                r.eu[rows, cols] = (d_up * scale).astype(bf16)
                both = d_gate * gate + d_up * up
                for j in range(0, 384, 128):
                    total = total + both[:, j : j + 128]
            r.lanes[here, :] = total

        in_rows(s, 16, body)
        sum_start(
            1,
            s,
            lambda n: nt(r.eg[rows_of(s), :], r.wg[part(n), :]) + nt(r.eu[rows_of(s), :], r.wu[part(n), :]),
        )
        totals_start(0, s, r.lanes[...])

    feed(0)
    feed(1)
    sum_relay(1, 0)
    grad_product(GATE, r.qg, r.eg)
    sum_relay(1, 1)

    small = r.sums.at[0]
    small[...] = jnp.zeros((8, CH), f32)

    def through_norm(s):
        sum_finish(1, s)
        totals_finish(0, s)

        def body(i, rows):
            g = summed(1, s, i, 32)
            value, scale = r.resid[rows, :], r.r2[rows, :]
            small[1:2, :] += jnp.sum(g * value, axis=0, keepdims=True)
            d = (
                r.cg[rows, part(t)].astype(f32)
                + fg[...] * g
                - value * (scale * scale * r.col[0, rows, :] * (1.0 / WIDE))
            )
            r.dres[rows, :] = d
            r.bg[rows, part(t)] = d.astype(bf16)

        in_rows(s, 32, body)
        gather_start(B, r.bg.at[rows_of(s), part(t)], s)

    through_norm(0)
    through_norm(1)
    grad_product(UP, r.qg, r.eu)
    gather_relay(B, 0)
    gather_relay(B, 1)
    grad_first(GATE)
    for s in range(2):
        sum_start(2, s, lambda n: nn(r.hid[rows_of(s), :], r.wd[:, part(n)]))

    def back(s):
        gather_finish(B, s)
        d = nt(r.bg[rows_of(s), :], r.wo[...])
        r.tg[:, 0:CH] = d
        for i in range(0, SEQ, 64):
            rows = pl.ds(s * SEQ + i, 64)
            d = r.tg[i : i + 64, 0:CH]
            d_conv = d * r.proj[1, rows, :]
            r.dpad[s, i : i + 64, :] = d_conv
            d_c = d * r.conv[rows, :]
            r.dproj[rows, CH : 2 * CH] = d_c.astype(bf16)
            for j in range(3):
                small[2 + j : 3 + j, :] += jnp.sum(
                    d_conv * r.mpad[s, i + 6 + j : i + 70 + j, :], axis=0, keepdims=True
                )
        r.ds[s] = r.dpad[s, 0:8, :]
        send((BACK, s), r.ds.at[s], r.dr.at[s], PREV)

    def mixer(s):
        arrived((BACK, s), r.dr.at[s])
        r.dpad[s, SEQ : SEQ + 8, :] = jnp.where(ctx < 15, r.dr[s], 0.0)
        for i in range(0, SEQ, 64):
            rows = pl.ds(s * SEQ + i, 64)
            d_mixed = (
                taps[2:3, :] * r.dpad[s, i : i + 64, :]
                + taps[1:2, :] * r.dpad[s, i + 1 : i + 65, :]
                + taps[0:1, :] * r.dpad[s, i + 2 : i + 66, :]
            )
            b, c, xi = r.proj[0, rows, :], r.proj[1, rows, :], r.proj[2, rows, :]
            d_b, d_x = (d_mixed * xi).astype(bf16), (d_mixed * b).astype(bf16)
            r.dproj[rows, 0:CH] = d_b
            r.dproj[rows, 2 * CH :] = d_x
            d_c = r.dproj[rows, CH : 2 * CH].astype(f32)
            both = d_b.astype(f32) * b + d_x.astype(f32) * xi + d_c * c
            r.lanes[i : i + 64, :] = both[:, 0:128] + both[:, 128:256]

        def term(n):
            total = nt(r.dproj[rows_of(s), 0:CH], r.wi[0, part(n), :])
            for k in (1, 2):
                total += nt(r.dproj[rows_of(s), k * CH : (k + 1) * CH], r.wi[k, part(n), :])
            return total

        sum_start(3, s, term)
        totals_start(1, s, r.lanes[...])

    grad_first(UP)
    back(0)
    back(1)
    grad_next(GATE, 1)
    mixer(0)
    mixer(1)
    grad_product(IN, r.n1, r.dproj)
    sum_relay(3, 0)
    sum_relay(3, 1)
    grad_next(UP, 1)
    grad_next(GATE, 2)
    grad_product(OUT, r.bg, r.gated)
    grad_product(DOWN, r.cg, r.hid)
    sum_relay(2, 0)
    sum_relay(2, 1)
    grad_first(IN)
    grad_first(OUT)
    grad_first(DOWN)
    grad_next(UP, 2)

    def finish(s):
        sum_finish(3, s)
        totals_finish(1, s)

        def body(i, rows):
            g = summed(3, s, i, 32)
            value, scale = r.xg[rows, part(t)].astype(f32), r.r1[rows, :]
            small[0:1, :] += jnp.sum(g * (value * scale), axis=0, keepdims=True)
            input_grad[rows, :] = (
                r.dres[rows, :]
                + scale * (mg[...] * g)
                - value * (scale * scale * r.col[1, rows, :] * (1.0 / WIDE))
            )

        in_rows(s, 32, body)

    finish(0)
    finish(1)
    hops = (CORE, Z1, Z3, X1, X3)

    def small_send(n):
        send((SMALL, n), r.sums.at[n], r.sumr.at[n], hops[n])

    def small_add(n):
        arrived((SMALL, n), r.sumr.at[n])
        r.sums[n + 1] = r.sums[n] + r.sumr[n]

    small_send(0)
    grad_next(IN, 1)
    grad_next(OUT, 1)
    grad_next(DOWN, 1)
    small_add(0)
    small_send(1)
    grad_next(GATE, 3)
    grad_next(UP, 3)
    small_add(1)
    small_send(2)
    grad_next(IN, 2)
    grad_next(OUT, 2)
    grad_next(DOWN, 2)
    for s in range(2):
        sum_finish(2, s)

        def body(i, rows):
            block_out[rows, :] = (r.resid[rows, :] + summed(2, s, i, 32)).astype(bf16)

        in_rows(s, 32, body)
    small_add(2)
    small_send(3)
    grad_last(GATE)
    grad_last(UP)
    grad_next(IN, 3)
    grad_next(OUT, 3)
    grad_next(DOWN, 3)
    small_add(3)
    small_send(4)
    grad_last(IN)
    grad_last(OUT)
    grad_last(DOWN)
    small_add(4)
    g_small[...] = r.sums[5]
    for copy in sent:
        copy.wait_send()


def on_device(block_input, in_proj, out_proj, gate_proj, up_proj, down_proj, mixer_gain, ffn_gain, conv_kernel, cotangent):
    shapes = scratch()

    def kernel(*refs):
        taken, held = refs[18:], {}
        count = 0
        for name, shape in shapes.items():
            if isinstance(shape, list):
                held[name] = taken[count : count + len(shape)]
                count += len(shape)
            else:
                held[name] = taken[count]
                count += 1
        block_kernel(types.SimpleNamespace(**held), *refs[:18])

    hbm, vmem = pl.BlockSpec(memory_space=pl.ANY), pl.BlockSpec(memory_space=pltpu.VMEM)
    out = jax.ShapeDtypeStruct
    (block_out, input_grad, g_in, g_out, g_gate, g_up, g_down, g_small) = pl.pallas_call(
        kernel,
        out_shape=(
            out((TOK, CH), bf16),
            out((TOK, CH), f32),
            out((3, 32, CH), f32),
            out((32, CH), f32),
            out((32, HID), f32),
            out((32, HID), f32),
            out((32, HID), f32),
            out((8, CH), f32),
        ),
        in_specs=[hbm] * 7 + [vmem] * 3,
        out_specs=[vmem] * 8,
        scratch_shapes=jax.tree.leaves(list(shapes.values())),
        compiler_params=pltpu.CompilerParams(
            collective_id=0, has_side_effects=True, vmem_limit_bytes=62 * 1024 * 1024
        ),
    )(
        block_input.reshape(TOK, CH),
        cotangent.reshape(TOK, CH),
        jnp.transpose(in_proj, (1, 0, 2)),
        out_proj,
        gate_proj,
        up_proj,
        down_proj,
        mixer_gain.reshape(1, CH),
        ffn_gain.reshape(1, CH),
        conv_kernel,
    )
    return (
        block_out.reshape(2, SEQ, CH),
        input_grad.reshape(2, SEQ, CH),
        jnp.transpose(g_in, (1, 0, 2)),
        g_out.T,
        g_gate,
        g_up,
        g_down.T,
        g_small[0],
        g_small[1],
        g_small[2:5],
    )


def solution(mesh):
    return jax.shard_map(
        on_device,
        mesh=mesh,
        in_specs=(
            P("shard", "ctx", "tp"),
            P("shard", None, "tp"),
            P("tp", "shard"),
            P("shard", "tp"),
            P("shard", "tp"),
            P("tp", "shard"),
            P("tp"),
            P("tp"),
            P(None, "tp"),
            P("shard", "ctx", "tp"),
        ),
        out_specs=(
            P("shard", "ctx", "tp"),
            P("shard", "ctx", "tp"),
            P(("shard", "ctx"), None, "tp"),
            P("tp", ("shard", "ctx")),
            P(("shard", "ctx"), "tp"),
            P(("shard", "ctx"), "tp"),
            P("tp", ("shard", "ctx")),
            P("tp"),
            P("tp"),
            P(None, "tp"),
        ),
        check_vma=False,
    )
```

```python
import types

import jax
import jax.numpy as jnp
from jax import lax
from jax.experimental import pallas as pl
from jax.experimental.pallas import tpu as pltpu
from jax.sharding import PartitionSpec as P

EPS = 1e-05
MESH = pl.DeviceIdType.MESH
f32, bf16 = jnp.float32, jnp.bfloat16
WIDE, SEQ, TOK, CH, HID = 1024, 256, 512, 256, 1152
DOWN, GATE, UP, OUT, IN = range(5)
COLS = (HID, HID, HID, CH, 3 * CH)
RIGHT, LEFT, ACROSS, CORE, Z1, X1, Z3, X3, NEXT, PREV, X2, Z2, Z1C, Z2C, Z3C = range(15)
AHEAD, GATHER, SUM, TOTAL, GRAD, GAINS, EDGE, BACK, SMALL = range(9)
X, COT, Q, B = range(5, 9)
def scratch():
    v = pltpu.VMEM
    shapes = dict(
        xg=v((TOK, WIDE), bf16),
        cg=v((TOK, WIDE), bf16),
        qg=v((TOK, WIDE), bf16),
        bg=v((TOK, WIDE), bf16),
        n1=v((TOK, WIDE), bf16),
        gains=v((8, WIDE), f32),
        r1=v((TOK, 1), f32),
        r2=v((TOK, 1), f32),
        col=v((2, TOK, 1), f32),
        wi=v((3, WIDE, CH), bf16),
        wo=v((CH, WIDE), bf16),
        wg=v((WIDE, HID), bf16),
        wu=v((WIDE, HID), bf16),
        wd=v((HID, WIDE), bf16),
        proj=v((3, TOK, CH), f32),
        mpad=v((2, SEQ + 8, CH), f32),
        hs=v((2, 16, CH), bf16),
        hr=v((2, 16, CH), bf16),
        conv=v((TOK, CH), f32),
        gated=v((TOK, CH), bf16),
        ys=v((4, 2, 3, SEQ, CH), bf16),
        yr=v((4, 2, 3, SEQ, CH), bf16),
        own=v((4, TOK, CH), f32),
        resid=v((TOK, CH), f32),
        tg=v((SEQ, HID), f32),
        tu=v((SEQ, HID), f32),
        td=v((SEQ, HID), f32),
        lanes=v((SEQ, 128), f32),
        hid=v((TOK, HID), bf16),
        eg=v((TOK, HID), bf16),
        eu=v((TOK, HID), bf16),
        dres=v((TOK, CH), f32),
        dpad=v((2, SEQ + 8, CH), f32),
        ds=v((2, 8, CH), f32),
        dr=v((2, 8, CH), f32),
        dproj=v((TOK, 3 * CH), bf16),
        rso=v((2, 2, 8, SEQ), f32),
        rsr=v((2, 2, 3, 8, SEQ), f32),
        sums=v((2, 8, CH), f32),
        sumr=v((10, 8, CH), f32),
        terms=[v((2, 2, 16, 16, n), bf16) for n in COLS],
        paired=[v((2, 16, 16, n), bf16) for n in COLS],
        came=[v((2, 15, 16, n), bf16) for n in COLS],
        ssem=pltpu.SemaphoreType.DMA((24,)),
        rsem=pltpu.SemaphoreType.DMA((64,)),
        lsem=pltpu.SemaphoreType.DMA((7,)),
    )
    return shapes


def nn(a, b):
    return jnp.dot(a, b, preferred_element_type=f32)


def nt(a, b):
    return lax.dot_general(a, b, (((1,), (1,)), ((), ())), preferred_element_type=f32)


def tn(a, b):
    return lax.dot_general(a, b, (((0,), (0,)), ((), ())), preferred_element_type=f32)


def row_of(lanes):
    ones = jnp.ones((8, lanes.shape[1]), f32)
    return lax.dot_general(
        ones, lanes, (((1,), (1,)), ((), ())), precision=lax.Precision.HIGHEST, preferred_element_type=f32
    )


def block_kernel(r, *refs):
    (x_hbm, cot_hbm, in_hbm, out_hbm, gate_hbm, up_hbm, down_hbm, mg, fg, taps) = refs[:10]
    (block_out, input_grad, g_in, g_out, g_gate, g_up, g_down, g_small) = refs[10:]
    grads = {DOWN: g_down, GATE: g_gate, UP: g_up, OUT: g_out, IN: g_in}
    ssem, rsem, lsem = r.ssem, r.rsem, r.lsem

    shard, ctx, t = lax.axis_index("shard"), lax.axis_index("ctx"), lax.axis_index("tp")
    core, z, x = ctx % 2, (ctx // 2) % 4, shard * 2 + ctx // 8

    def dev(xx, zz, cc, tt):
        return (xx // 2, (xx % 2) * 8 + zz * 2 + cc, tt)

    z1, z3, x1, x3 = z + 1 - 2 * (z % 2), 3 - z, x + 1 - 2 * (x % 2), 3 - x
    right, left, across = (t + 1) % 4, (t + 3) % 4, (t + 2) % 4
    to = {
        RIGHT: (shard, ctx, right),
        LEFT: (shard, ctx, left),
        ACROSS: (shard, ctx, across),
        CORE: dev(x, z, 1 - core, t),
        Z1: dev(x, z1, core, t),
        Z3: dev(x, z3, core, t),
        X1: dev(x1, z, core, t),
        X3: dev(x3, z, core, t),
        NEXT: (shard, (ctx + 1) % 16, t),
        PREV: (shard, (ctx + 15) % 16, t),
        X2: dev((x + 2) % 4, z, core, t),
        Z2: dev(x, (z + 2) % 4, core, t),
        Z1C: dev(x, z1, 1 - core, t),
        Z2C: dev(x, (z + 2) % 4, 1 - core, t),
        Z3C: dev(x, z3, 1 - core, t),
    }

    came_ids, sent_ids, local = {}, {}, {}
    gathered = {X: r.xg, COT: r.cg, Q: r.qg, B: r.bg}

    def send(key, group, src, dst, where):
        n, m = came_ids.setdefault(key, len(came_ids)), sent_ids.setdefault(group, len(sent_ids))
        pltpu.make_async_remote_copy(
            src_ref=src,
            dst_ref=dst,
            send_sem=ssem.at[m],
            recv_sem=rsem.at[n],
            device_id=to[where],
            device_id_type=MESH,
        ).start()

    def arrived(key, size):
        pltpu.make_async_copy(size, size, rsem.at[came_ids[key]]).wait()

    def left_all(group, size):
        pltpu.make_async_copy(size, size, ssem.at[sent_ids[group]]).wait()

    def fetch(key, src, dst):
        copy = pltpu.make_async_copy(src, dst, lsem.at[len(local)])
        copy.start()
        local[key] = copy

    def part(n):
        return pl.ds(pl.multiple_of(n * CH, CH), CH)

    def rows_of(s):
        return pl.ds(s * SEQ, SEQ)

    weights = {
        IN: (in_hbm, r.wi, 512),
        OUT: (out_hbm, r.wo, 256),
        GATE: (gate_hbm, r.wg, 512),
        UP: (up_hbm, r.wu, 512),
        DOWN: (down_hbm, r.wd, HID),
    }

    def piece(w, half, first, count):
        whole = weights[w][1]
        if w == IN:
            return whole.at[:, pl.ds(pl.multiple_of(half * 512 + first, 32), count), :]
        if w in (GATE, UP):
            return whole.at[pl.ds(pl.multiple_of(half * 512 + first, 32), count), :]
        return whole.at[pl.ds(pl.multiple_of(first, 16), count), pl.ds(pl.multiple_of(half * 512, 512), 512)]

    def source(w, first, count):
        held = weights[w][0]
        at = pl.ds(pl.multiple_of(first, 16), count)
        return held.at[:, at, :] if w == IN else held.at[at, :]

    def quarter(w):
        return weights[w][2] // 4

    pair = z % 2

    def weight_own(w):
        fetch(w, weights[w][0], piece(w, shard, 0, weights[w][2]))

    def weight_cross(w):
        n = quarter(w)
        first = (pair * 2 + core) * n
        send((AHEAD, w, 0), (AHEAD, w), source(w, first, n), piece(w, shard, first, n), X3)

    def weight_around(w):
        n = quarter(w)
        first = (pair * 2 + core) * n
        mine = piece(w, 1 - shard, first, n)
        arrived((AHEAD, w, 0), mine)
        a, b = piece(w, 1 - shard, first, n // 2), piece(w, 1 - shard, first + n // 2, n // 2)
        send((AHEAD, w, 1), (AHEAD, w), a, a, Z1)
        send((AHEAD, w, 1), (AHEAD, w), b, b, Z3)
        send((AHEAD, w, 2), (AHEAD, w), mine, mine, CORE)

    def weight_share(w):
        n = quarter(w)
        first = ((1 - pair) * 2 + core) * n
        other = piece(w, 1 - shard, first, n)
        arrived((AHEAD, w, 1), other)
        send((AHEAD, w, 2), (AHEAD, w), other, other, CORE)

    def weight_ready(w):
        arrived((AHEAD, w, 2), piece(w, 1 - shard, 0, 2 * quarter(w)))
        local[w].wait()

    others = ((ACROSS, across), (RIGHT, right), (LEFT, left))

    def gather_start(name, src, s):
        dst = gathered[name].at[rows_of(s), part(t)]
        for where, _ in others:
            send((GATHER, name, s), GATHER, src, dst, where)

    def gather_finish(name, s):
        arrived((GATHER, name, s), r.ys.at[0, 0])

    def ring_start(name, src, s):
        dst = gathered[name].at[rows_of(s), part(t)]
        send((GATHER, name, s, RIGHT), name, src, dst, RIGHT)
        send((GATHER, name, s, LEFT), name, src, dst, LEFT)

    def ring_relay(name, s):
        whole = gathered[name]
        arrived((GATHER, name, s, RIGHT), whole.at[rows_of(s), part(left)])
        a = whole.at[pl.ds(s * SEQ, SEQ // 2), part(left)]
        send((GATHER, name, s, X1), name, a, a, RIGHT)
        arrived((GATHER, name, s, LEFT), whole.at[rows_of(s), part(right)])
        b = whole.at[pl.ds(s * SEQ + SEQ // 2, SEQ // 2), part(right)]
        send((GATHER, name, s, X3), name, b, b, LEFT)

    def ring_finish(name, s):
        whole = gathered[name]
        arrived((GATHER, name, s, X1), whole.at[pl.ds(s * SEQ, SEQ // 2), part(across)])
        arrived((GATHER, name, s, X3), whole.at[pl.ds(s * SEQ + SEQ // 2, SEQ // 2), part(across)])

    def sum_start(ph, s, block):
        for slot, (where, n) in enumerate(others):
            r.ys[ph, s, slot] = block(n).astype(bf16)
            send((SUM, ph, s), SUM, r.ys.at[ph, s, slot], r.yr.at[ph, s, slot], where)
        r.own[ph, rows_of(s), :] = block(t)

    def sum_finish(ph, s):
        arrived((SUM, ph, s), r.yr.at[ph, s])

    def summed(ph, s, i, n):
        total = r.own[ph, pl.ds(s * SEQ + i, n), :]
        for slot in range(3):
            total = total + r.yr[ph, s, slot, pl.ds(i, n), :].astype(f32)
        return total

    def totals_start(kind, s, lanes):
        r.rso[kind, s] = row_of(lanes)
        for slot, where in enumerate((RIGHT, LEFT, ACROSS)):
            send((TOTAL, kind, s), TOTAL, r.rso.at[kind, s], r.rsr.at[kind, s, slot], where)

    def totals_finish(kind, s):
        total = r.rso[kind, s]
        arrived((TOTAL, kind, s), r.rsr.at[kind, s])
        for slot in range(3):
            total = total + r.rsr[kind, s, slot]
        r.col[kind, rows_of(s), :] = jnp.transpose(total)[:, 0:1]

    def grad_product(g, lhs, rhs):
        held, width = r.terms[g], COLS[g]

        @pl.loop(0, 4)
        def _(xp):
            a = lhs[:, part(xp)]
            xr = 2 * ((xp // 2 + x // 2) % 2) + (xp + x) % 2
            for first in range(0, width, 256):
                n = min(256, width - first)
                value = tn(a, rhs[:, first : first + n]).astype(bf16)
                for zp in range(4):
                    zr = 2 * ((zp // 2 + z // 2) % 2) + (zp + z) % 2
                    for cp in range(2):
                        mine = (cp + core) % 2
                        at = (zp * 2 + cp) * 32
                        held[mine, 0, 4 * zr + xr, :, first : first + n] = value[at : at + 16]
                        held[mine, 1, 4 * xr + zr, :, first : first + n] = value[at + 16 : at + 32]

        send((GRAD, g, 0), (GRAD, g, 0), held.at[1], r.paired[g], CORE)

    routes = (((Z1, Z2, Z3), (X1, X2, X3)), ((X1, X2, X3), (Z1, Z2, Z3)))

    def grad_first(g):
        held, came = r.terms[g], r.paired[g]
        arrived((GRAD, g, 0), came)

        @pl.loop(0, 16)
        def _(i):
            for half in range(2):
                held[0, half, i] = (held[0, half, i].astype(f32) + came[half, i].astype(f32)).astype(bf16)

        for n in (2, 1, 3):
            for half in range(2):
                send(
                    (GRAD, g, 1),
                    (GRAD, g, 1),
                    held.at[0, half, pl.ds(4 * n, 4)],
                    r.came[g].at[half, pl.ds(4 * n - 4, 4)],
                    routes[half][0][n - 1],
                )

    def grad_second(g):
        held, came = r.terms[g], r.came[g]
        arrived((GRAD, g, 1), came.at[:, pl.ds(0, 12)])

        @pl.loop(0, 4)
        def _(i):
            for half in range(2):
                total = held[0, half, i].astype(f32)
                for n in range(3):
                    total = total + came[half, 4 * n + i].astype(f32)
                held[0, half, i] = total.astype(bf16)

        for n in (2, 1, 3):
            for half in range(2):
                send(
                    (GRAD, g, 2),
                    (GRAD, g, 1),
                    held.at[0, half, pl.ds(n, 1)],
                    came.at[half, pl.ds(11 + n, 1)],
                    routes[half][1][n - 1],
                )

    def grad_last(g):
        held, came = r.terms[g], r.came[g]
        arrived((GRAD, g, 2), came.at[:, pl.ds(12, 3)])
        for half in range(2):
            total = held[0, half, 0].astype(f32)
            for n in range(12, 15):
                total = total + came[half, n].astype(f32)
            rows = pl.ds(half * 16, 16)
            if g == IN:
                for k in range(3):
                    g_in[k, rows, :] = total[:, k * CH : (k + 1) * CH]
            else:
                grads[g][rows, :] = total

    def in_rows(s, step, body):
        @pl.loop(0, SEQ // step)
        def _(n):
            i = pl.multiple_of(n * step, step)
            body(i, pl.ds(pl.multiple_of(s * SEQ + i, step), step))

    barrier = pltpu.get_barrier_semaphore()
    for where in to:
        pl.semaphore_signal(barrier, inc=1, device_id=to[where], device_id_type=MESH)
    fetch(X, x_hbm, r.xg.at[:, part(t)])
    fetch(COT, cot_hbm, r.cg.at[:, part(t)])
    for w in (IN, OUT, GATE, UP, DOWN):
        weight_own(w)
    own_gains = r.gains.at[:, part(t)]
    own_gains[...] = jnp.zeros((8, CH), f32)
    own_gains[0:1, :] = mg[...]
    own_gains[1:2, :] = fg[...]
    pl.semaphore_wait(barrier, len(to))

    weight_cross(IN)
    gather_start(X, x_hbm.at[rows_of(0)], 0)
    for where in (RIGHT, LEFT, ACROSS):
        send(GAINS, GAINS, own_gains, own_gains, where)
    gather_start(X, x_hbm.at[rows_of(1)], 1)
    for w in (OUT, GATE, UP, DOWN):
        weight_cross(w)
    for s in range(2):
        ring_start(COT, cot_hbm.at[rows_of(s)], s)
    weight_around(IN)

    def normalise(s):
        def body(i, rows):
            v = r.xg[rows, :].astype(f32)
            scale = lax.rsqrt(jnp.sum(v * v, axis=1, keepdims=True) / WIDE + EPS)
            r.r1[rows, :] = scale
            r.n1[rows, :] = (v * scale * r.gains[0:1, :]).astype(bf16)

        in_rows(s, 32, body)

    def project(s):
        for k in range(3):
            r.proj[k, rows_of(s), :] = nn(r.n1[rows_of(s), :], r.wi[k])
        mixed = (r.proj[0, rows_of(s), :] * r.proj[2, rows_of(s), :]).astype(bf16)
        r.mpad[s, pl.ds(8, SEQ), :] = mixed.astype(f32)
        r.hs[s] = mixed[SEQ - 16 :]
        send((EDGE, s), EDGE, r.hs.at[s], r.hr.at[s], NEXT)

    local[X].wait()
    arrived(GAINS, r.rsr.at[0, 0])
    gather_finish(X, 0)
    normalise(0)
    weight_share(IN)
    weight_around(OUT)
    weight_ready(IN)
    project(0)
    gather_finish(X, 1)
    normalise(1)
    project(1)
    weight_share(OUT)
    weight_around(GATE)

    def branch(s):
        arrived((EDGE, s), r.hr.at[s])
        edge = r.hr[s].astype(f32)[8:16]
        r.mpad[s, 0:8, :] = jnp.where(ctx > 0, edge, 0.0)

        for i in range(0, SEQ, 64):
            rows = pl.ds(s * SEQ + i, 64)
            c = (
                taps[0:1, :] * r.mpad[s, i + 6 : i + 70, :]
                + taps[1:2, :] * r.mpad[s, i + 7 : i + 71, :]
                + taps[2:3, :] * r.mpad[s, i + 8 : i + 72, :]
            )
            r.conv[rows, :] = c
            r.gated[rows, :] = (r.proj[1, rows, :] * c).astype(bf16)

        sum_start(0, s, lambda n: nn(r.gated[rows_of(s), :], r.wo[:, part(n)]))

    weight_ready(OUT)
    branch(0)
    branch(1)
    ring_relay(COT, 0)
    ring_relay(COT, 1)
    weight_around(UP)
    weight_share(GATE)

    def second(s):
        sum_finish(0, s)

        def body(i, rows):
            value = r.xg[rows, part(t)].astype(f32) + summed(0, s, i, 32)
            r.resid[rows, :] = value
            r.qg[rows, part(t)] = (value * fg[...]).astype(bf16)

        in_rows(s, 32, body)
        gather_start(Q, r.qg.at[rows_of(s), part(t)], s)

    second(0)
    second(1)
    weight_around(DOWN)
    weight_share(UP)
    local[COT].wait()

    def feed(s):
        gather_finish(Q, s)

        def scales(i, rows):
            v = r.qg[rows, :].astype(f32) * (1.0 / r.gains[1:2, :])
            r.r2[rows, :] = lax.rsqrt(jnp.sum(v * v, axis=1, keepdims=True) / WIDE + EPS)

        in_rows(s, 32, scales)
        if s == 0:
            weight_ready(GATE)
        q = r.qg[rows_of(s), :]
        slices = [pl.ds(first, min(256, HID - first)) for first in range(0, HID, 256)]
        for cols in slices:
            r.tg[:, cols] = nn(q, r.wg[:, cols])
        if s == 0:
            weight_share(DOWN)
            weight_ready(UP)
        for cols in slices:
            r.tu[:, cols] = nn(q, r.wu[:, cols])
        ring_finish(COT, s)
        if s == 0:
            weight_ready(DOWN)
        c = r.cg[rows_of(s), :]
        for cols in slices:
            r.td[:, cols] = nt(c, r.wd[cols, :])

        def body(i, rows):
            here = pl.ds(i, 16)
            scale = r.r2[rows, :]
            total = jnp.zeros((16, 128), f32)
            for first in range(0, HID, 384):
                cols = pl.ds(first, 384)
                gate, up, dh = r.tg[here, cols] * scale, r.tu[here, cols] * scale, r.td[here, cols]
                sg = jax.nn.sigmoid(gate)
                act = gate * sg
                r.hid[rows, cols] = (act * up).astype(bf16)
                d_gate = dh * up * sg * (1.0 + gate * (1.0 - sg))
                d_up = dh * act
                r.eg[rows, cols] = (d_gate * scale).astype(bf16)
                r.eu[rows, cols] = (d_up * scale).astype(bf16)
                both = d_gate * gate + d_up * up
                for j in range(0, 384, 128):
                    total = total + both[:, j : j + 128]
            r.lanes[here, :] = total

        in_rows(s, 16, body)
        sum_start(
            1,
            s,
            lambda n: nt(r.eg[rows_of(s), :], r.wg[part(n), :]) + nt(r.eu[rows_of(s), :], r.wu[part(n), :]),
        )
        totals_start(0, s, r.lanes[...])

    feed(0)
    feed(1)

    small = r.sums.at[0]
    small[...] = jnp.zeros((8, CH), f32)

    def through_norm(s):
        sum_finish(1, s)
        totals_finish(0, s)

        def body(i, rows):
            g = summed(1, s, i, 32)
            value, scale = r.resid[rows, :], r.r2[rows, :]
            small[1:2, :] += jnp.sum(g * value, axis=0, keepdims=True)
            d = (
                r.cg[rows, part(t)].astype(f32)
                + fg[...] * g
                - value * (scale * scale * r.col[0, rows, :] * (1.0 / WIDE))
            )
            r.dres[rows, :] = d
            r.bg[rows, part(t)] = d.astype(bf16)

        in_rows(s, 32, body)
        gather_start(B, r.bg.at[rows_of(s), part(t)], s)

    through_norm(0)
    grad_product(GATE, r.qg, r.eg)
    grad_product(UP, r.qg, r.eu)
    through_norm(1)

    def deliver(s):
        sum_start(2, s, lambda n: nn(r.hid[rows_of(s), :], r.wd[:, part(n)]))

    deliver(0)
    grad_first(GATE)

    def back(s):
        gather_finish(B, s)
        d = nt(r.bg[rows_of(s), :], r.wo[...])
        r.tg[:, 0:CH] = d
        for i in range(0, SEQ, 64):
            rows = pl.ds(s * SEQ + i, 64)
            d = r.tg[i : i + 64, 0:CH]
            d_conv = d * r.proj[1, rows, :]
            r.dpad[s, i : i + 64, :] = d_conv
            d_c = d * r.conv[rows, :]
            r.dproj[rows, CH : 2 * CH] = d_c.astype(bf16)
            for j in range(3):
                small[2 + j : 3 + j, :] += jnp.sum(
                    d_conv * r.mpad[s, i + 6 + j : i + 70 + j, :], axis=0, keepdims=True
                )
        r.ds[s] = r.dpad[s, 0:8, :]
        send((BACK, s), BACK, r.ds.at[s], r.dr.at[s], PREV)

    def mixer(s):
        arrived((BACK, s), r.dr.at[s])
        r.dpad[s, SEQ : SEQ + 8, :] = jnp.where(ctx < 15, r.dr[s], 0.0)
        for i in range(0, SEQ, 64):
            rows = pl.ds(s * SEQ + i, 64)
            d_mixed = (
                taps[2:3, :] * r.dpad[s, i : i + 64, :]
                + taps[1:2, :] * r.dpad[s, i + 1 : i + 65, :]
                + taps[0:1, :] * r.dpad[s, i + 2 : i + 66, :]
            )
            b, c, xi = r.proj[0, rows, :], r.proj[1, rows, :], r.proj[2, rows, :]
            d_b, d_x = (d_mixed * xi).astype(bf16), (d_mixed * b).astype(bf16)
            r.dproj[rows, 0:CH] = d_b
            r.dproj[rows, 2 * CH :] = d_x
            d_c = r.dproj[rows, CH : 2 * CH].astype(f32)
            both = d_b.astype(f32) * b + d_x.astype(f32) * xi + d_c * c
            r.lanes[i : i + 64, :] = both[:, 0:128] + both[:, 128:256]

        def term(n):
            total = nt(r.dproj[rows_of(s), 0:CH], r.wi[0, part(n), :])
            for k in (1, 2):
                total += nt(r.dproj[rows_of(s), k * CH : (k + 1) * CH], r.wi[k, part(n), :])
            return total

        sum_start(3, s, term)
        totals_start(1, s, r.lanes[...])

    back(0)
    grad_product(DOWN, r.cg, r.hid)
    grad_first(UP)
    mixer(0)
    back(1)
    grad_product(OUT, r.bg, r.gated)
    grad_second(GATE)
    grad_first(DOWN)
    mixer(1)
    grad_product(IN, r.n1, r.dproj)
    deliver(1)
    grad_second(UP)
    grad_first(OUT)

    def finish(s):
        sum_finish(3, s)
        totals_finish(1, s)

        def body(i, rows):
            g = summed(3, s, i, 32)
            value, scale = r.xg[rows, part(t)].astype(f32), r.r1[rows, :]
            small[0:1, :] += jnp.sum(g * (value * scale), axis=0, keepdims=True)
            input_grad[rows, :] = (
                r.dres[rows, :]
                + scale * (mg[...] * g)
                - value * (scale * scale * r.col[1, rows, :] * (1.0 / WIDE))
            )

        in_rows(s, 32, body)

    finish(0)
    grad_first(IN)
    grad_second(DOWN)
    grad_last(GATE)
    finish(1)
    for n, where in enumerate((CORE, Z1, Z2, Z3, Z1C, Z2C, Z3C)):
        send((SMALL, 0), SMALL, r.sums.at[0], r.sumr.at[n], where)
    grad_second(OUT)
    grad_last(UP)
    for s in range(2):
        sum_finish(2, s)

        def body(i, rows):
            block_out[rows, :] = (r.resid[rows, :] + summed(2, s, i, 32)).astype(bf16)

        in_rows(s, 32, body)
    total = r.sums[0]
    arrived((SMALL, 0), r.sumr.at[pl.ds(0, 7)])
    for n in range(7):
        total = total + r.sumr[n]
    r.sums[1] = total
    for n, where in enumerate((X1, X2, X3)):
        send((SMALL, 1), SMALL, r.sums.at[1], r.sumr.at[7 + n], where)
    grad_second(IN)
    grad_last(DOWN)
    grad_last(OUT)
    arrived((SMALL, 1), r.sumr.at[pl.ds(7, 3)])
    for n in range(7, 10):
        total = total + r.sumr[n]
    g_small[...] = total
    grad_last(IN)

    left_all(SUM, r.ys)
    left_all(GATHER, r.ys.at[pl.ds(0, 3)])
    left_all(COT, r.ys.at[0])
    left_all(TOTAL, r.rsr)
    left_all(GAINS, r.rsr.at[0, 0])
    left_all(SMALL, r.sumr)
    left_all(EDGE, r.hr)
    left_all(BACK, r.dr)
    for w in (IN, OUT, GATE, UP, DOWN):
        left_all((AHEAD, w), piece(w, 0, 0, weights[w][2]))
        left_all((GRAD, w, 0), r.paired[w])
        left_all((GRAD, w, 1), r.came[w])


def deliver_kernel(*refs):
    small, whole = refs[0], refs[1:8]
    ends, sums = refs[8:15], refs[15:18]
    held, sem = refs[18:25], refs[25]
    taken = [pltpu.make_async_copy(a, b, sem.at[0, n]) for n, (a, b) in enumerate(zip(whole, held))]
    copies = [pltpu.make_async_copy(a, b, sem.at[1, n]) for n, (a, b) in enumerate(zip(held, ends))]
    for copy in taken:
        copy.start()
    for first, then in zip(taken, copies):
        first.wait()
        then.start()
    sums[0][...] = small[0]
    sums[1][...] = small[1]
    sums[2][...] = small[2:5]
    for copy in copies:
        copy.wait()


def on_device(block_input, in_proj, out_proj, gate_proj, up_proj, down_proj, mixer_gain, ffn_gain, conv_kernel, cotangent):
    shapes = scratch()

    def kernel(*refs):
        taken, held = refs[18:], {}
        count = 0
        for name, shape in shapes.items():
            if isinstance(shape, list):
                held[name] = taken[count : count + len(shape)]
                count += len(shape)
            else:
                held[name] = taken[count]
                count += 1
        block_kernel(types.SimpleNamespace(**held), *refs[:18])

    hbm, vmem = pl.BlockSpec(memory_space=pl.ANY), pl.BlockSpec(memory_space=pltpu.VMEM)
    out = jax.ShapeDtypeStruct
    *whole, small = pl.pallas_call(
        kernel,
        out_shape=(
            out((TOK, CH), bf16),
            out((TOK, CH), f32),
            out((3, 32, CH), f32),
            out((32, CH), f32),
            out((32, HID), f32),
            out((32, HID), f32),
            out((32, HID), f32),
            out((8, CH), f32),
        ),
        in_specs=[hbm] * 7 + [vmem] * 3,
        out_specs=[vmem] * 8,
        scratch_shapes=jax.tree.leaves(list(shapes.values())),
        compiler_params=pltpu.CompilerParams(
            collective_id=0, has_side_effects=True, vmem_limit_bytes=62 * 1024 * 1024
        ),
    )(
        block_input.reshape(TOK, CH),
        cotangent.reshape(TOK, CH),
        jnp.transpose(in_proj, (1, 0, 2)),
        out_proj,
        gate_proj,
        up_proj,
        down_proj,
        mixer_gain.reshape(1, CH),
        ffn_gain.reshape(1, CH),
        conv_kernel,
    )
    block_out, input_grad, g_in, g_out, g_gate, g_up, g_down, mixer_sum, ffn_sum, taps_sum = pl.pallas_call(
        deliver_kernel,
        out_shape=(
            *(out(a.shape, a.dtype) for a in whole),
            out((CH,), f32),
            out((CH,), f32),
            out((3, CH), f32),
        ),
        in_specs=[vmem] + [hbm] * 7,
        out_specs=[hbm] * 7 + [vmem] * 3,
        scratch_shapes=[pltpu.VMEM(a.shape, a.dtype) for a in whole] + [pltpu.SemaphoreType.DMA((2, 7))],
    )(small, *whole)
    return (
        block_out.reshape(2, SEQ, CH),
        input_grad.reshape(2, SEQ, CH),
        jnp.transpose(g_in, (1, 0, 2)),
        g_out.T,
        g_gate,
        g_up,
        g_down.T,
        mixer_sum,
        ffn_sum,
        taps_sum,
    )


def solution(mesh):
    return jax.shard_map(
        on_device,
        mesh=mesh,
        in_specs=(
            P("shard", "ctx", "tp"),
            P("shard", None, "tp"),
            P("tp", "shard"),
            P("shard", "tp"),
            P("shard", "tp"),
            P("tp", "shard"),
            P("tp"),
            P("tp"),
            P(None, "tp"),
            P("shard", "ctx", "tp"),
        ),
        out_specs=(
            P("shard", "ctx", "tp"),
            P("shard", "ctx", "tp"),
            P(("shard", "ctx"), None, "tp"),
            P("tp", ("shard", "ctx")),
            P(("shard", "ctx"), "tp"),
            P(("shard", "ctx"), "tp"),
            P("tp", ("shard", "ctx")),
            P("tp"),
            P("tp"),
            P(None, "tp"),
        ),
        check_vma=False,
    )
```

```python
import types

import jax
import jax.numpy as jnp
from jax import lax
from jax.experimental import pallas as pl
from jax.experimental.pallas import tpu as pltpu
from jax.sharding import PartitionSpec as P

EPS = 1e-05
MESH = pl.DeviceIdType.MESH
f32, bf16 = jnp.float32, jnp.bfloat16
WIDE, SEQ, TOK, CH, HID = 1024, 256, 512, 256, 1152
DOWN, GATE, UP, OUT, IN = range(5)
COLS = (HID, HID, HID, CH, 3 * CH)
RIGHT, LEFT, ACROSS, CORE, Z1, X1, Z3, X3, NEXT, PREV, X2, Z2, Z1C, Z2C, Z3C = range(15)
AHEAD, GATHER, SUM, TOTAL, GRAD, GAINS, EDGE, BACK, SMALL = range(9)
X, COT, Q, B = range(20, 24)
def scratch():
    v = pltpu.VMEM
    shapes = dict(
        xg=v((TOK, WIDE), bf16),
        cg=v((TOK, WIDE), bf16),
        qg=v((TOK, WIDE), bf16),
        bg=v((TOK, WIDE), bf16),
        n1=v((TOK, WIDE), bf16),
        gains=v((8, WIDE), f32),
        r1=v((TOK, 1), f32),
        r2=v((TOK, 1), f32),
        col=v((2, TOK, 1), f32),
        wi=v((3, WIDE, CH), bf16),
        wo=v((CH, WIDE), bf16),
        wg=v((WIDE, HID), bf16),
        wu=v((WIDE, HID), bf16),
        wd=v((HID, WIDE), bf16),
        proj=v((3, TOK, CH), f32),
        mpad=v((2, SEQ + 8, CH), f32),
        hs=v((2, 16, CH), bf16),
        hr=v((2, 16, CH), bf16),
        conv=v((TOK, CH), f32),
        gated=v((TOK, CH), bf16),
        ys=v((4, 2, 3, SEQ, CH), bf16),
        yr=v((4, 2, 3, SEQ, CH), bf16),
        own=v((4, TOK, CH), f32),
        resid=v((TOK, CH), f32),
        tg=v((SEQ, HID), f32),
        tu=v((SEQ, HID), f32),
        td=v((SEQ, HID), f32),
        lanes=v((SEQ, 128), f32),
        hid=v((TOK, HID), bf16),
        eg=v((TOK, HID), bf16),
        eu=v((TOK, HID), bf16),
        dres=v((TOK, CH), f32),
        dpad=v((2, SEQ + 8, CH), f32),
        ds=v((2, 8, CH), f32),
        dr=v((2, 8, CH), f32),
        dproj=v((TOK, 3 * CH), bf16),
        rso=v((2, 2, 8, SEQ), f32),
        rsr=v((2, 2, 3, 8, SEQ), f32),
        sums=v((2, 8, CH), f32),
        sumr=v((10, 8, CH), f32),
        terms=[v((2, 2, 16, 16, n), bf16) for n in COLS],
        paired=[v((2, 16, 16, n), bf16) for n in COLS],
        came=[v((2, 15, 16, n), bf16) for n in COLS],
        ssem=pltpu.SemaphoreType.DMA((24,)),
        rsem=pltpu.SemaphoreType.DMA((64,)),
        lsem=pltpu.SemaphoreType.DMA((7,)),
    )
    return shapes


def nn(a, b):
    return jnp.dot(a, b, preferred_element_type=f32)


def nt(a, b):
    return lax.dot_general(a, b, (((1,), (1,)), ((), ())), preferred_element_type=f32)


def tn(a, b):
    return lax.dot_general(a, b, (((0,), (0,)), ((), ())), preferred_element_type=f32)


def row_of(lanes):
    ones = jnp.ones((8, lanes.shape[1]), f32)
    return lax.dot_general(
        ones, lanes, (((1,), (1,)), ((), ())), precision=lax.Precision.HIGHEST, preferred_element_type=f32
    )


def block_kernel(r, *refs):
    (x_hbm, cot_hbm, in_hbm, out_hbm, gate_hbm, up_hbm, down_hbm, mg, fg, taps) = refs[:10]
    (block_out, input_grad, g_in, g_out, g_gate, g_up, g_down, g_small) = refs[10:]
    grads = {DOWN: g_down, GATE: g_gate, UP: g_up, OUT: g_out, IN: g_in}
    ssem, rsem, lsem = r.ssem, r.rsem, r.lsem

    shard, ctx, t = lax.axis_index("shard"), lax.axis_index("ctx"), lax.axis_index("tp")
    core, z, x = ctx % 2, (ctx // 2) % 4, shard * 2 + ctx // 8

    def dev(xx, zz, cc, tt):
        return (xx // 2, (xx % 2) * 8 + zz * 2 + cc, tt)

    z1, z3, x1, x3 = z + 1 - 2 * (z % 2), 3 - z, x + 1 - 2 * (x % 2), 3 - x
    right, left, across = (t + 1) % 4, (t + 3) % 4, (t + 2) % 4
    to = {
        RIGHT: (shard, ctx, right),
        LEFT: (shard, ctx, left),
        ACROSS: (shard, ctx, across),
        CORE: dev(x, z, 1 - core, t),
        Z1: dev(x, z1, core, t),
        Z3: dev(x, z3, core, t),
        X1: dev(x1, z, core, t),
        X3: dev(x3, z, core, t),
        NEXT: (shard, (ctx + 1) % 16, t),
        PREV: (shard, (ctx + 15) % 16, t),
        X2: dev((x + 2) % 4, z, core, t),
        Z2: dev(x, (z + 2) % 4, core, t),
        Z1C: dev(x, z1, 1 - core, t),
        Z2C: dev(x, (z + 2) % 4, 1 - core, t),
        Z3C: dev(x, z3, 1 - core, t),
    }

    came_ids, sent_ids, local = {}, {}, {}
    gathered = {X: r.xg, COT: r.cg, Q: r.qg, B: r.bg}

    def send(key, group, src, dst, where):
        n, m = came_ids.setdefault(key, len(came_ids)), sent_ids.setdefault(group, len(sent_ids))
        pltpu.make_async_remote_copy(
            src_ref=src,
            dst_ref=dst,
            send_sem=ssem.at[m],
            recv_sem=rsem.at[n],
            device_id=to[where],
            device_id_type=MESH,
        ).start()

    def arrived(key, size):
        pltpu.make_async_copy(size, size, rsem.at[came_ids[key]]).wait()

    def left_all(group, size):
        pltpu.make_async_copy(size, size, ssem.at[sent_ids[group]]).wait()

    def fetch(key, src, dst):
        copy = pltpu.make_async_copy(src, dst, lsem.at[len(local)])
        copy.start()
        local[key] = copy

    def part(n):
        return pl.ds(pl.multiple_of(n * CH, CH), CH)

    def rows_of(s):
        return pl.ds(s * SEQ, SEQ)

    weights = {
        IN: (in_hbm, r.wi, 512),
        OUT: (out_hbm, r.wo, 256),
        GATE: (gate_hbm, r.wg, 512),
        UP: (up_hbm, r.wu, 512),
        DOWN: (down_hbm, r.wd, HID),
    }

    def piece(w, half, first, count):
        whole = weights[w][1]
        if w == IN:
            return whole.at[:, pl.ds(pl.multiple_of(half * 512 + first, 32), count), :]
        if w in (GATE, UP):
            return whole.at[pl.ds(pl.multiple_of(half * 512 + first, 32), count), :]
        return whole.at[pl.ds(pl.multiple_of(first, 16), count), pl.ds(pl.multiple_of(half * 512, 512), 512)]

    def source(w, first, count):
        held = weights[w][0]
        at = pl.ds(pl.multiple_of(first, 16), count)
        return held.at[:, at, :] if w == IN else held.at[at, :]

    def quarter(w):
        return weights[w][2] // 4

    pair = z % 2

    def weight_own(w):
        fetch(w, weights[w][0], piece(w, shard, 0, weights[w][2]))

    def weight_cross(w):
        n = quarter(w)
        first = (pair * 2 + core) * n
        send((AHEAD, w, 0), (AHEAD, w), source(w, first, n), piece(w, shard, first, n), X3)

    def weight_around(w):
        n = quarter(w)
        first = (pair * 2 + core) * n
        mine = piece(w, 1 - shard, first, n)
        arrived((AHEAD, w, 0), mine)
        a, b = piece(w, 1 - shard, first, n // 2), piece(w, 1 - shard, first + n // 2, n // 2)
        send((AHEAD, w, 1), (AHEAD, w), a, a, Z1)
        send((AHEAD, w, 1), (AHEAD, w), b, b, Z3)
        send((AHEAD, w, 2), (AHEAD, w), mine, mine, CORE)

    def weight_share(w):
        n = quarter(w)
        first = ((1 - pair) * 2 + core) * n
        other = piece(w, 1 - shard, first, n)
        arrived((AHEAD, w, 1), other)
        send((AHEAD, w, 2), (AHEAD, w), other, other, CORE)

    def weight_ready(w):
        arrived((AHEAD, w, 2), piece(w, 1 - shard, 0, 2 * quarter(w)))
        local[w].wait()

    others = ((RIGHT, right), (LEFT, left), (ACROSS, across))

    def gather_start(name, src, s):
        dst = gathered[name].at[rows_of(s), part(t)]
        for where, _ in others:
            send((GATHER, name, s), GATHER, src, dst, where)

    def gather_finish(name, s):
        arrived((GATHER, name, s), r.ys.at[0, 0])

    def ring_start(name, src, s):
        dst = gathered[name].at[rows_of(s), part(t)]
        send((GATHER, name, s, RIGHT), name, src, dst, RIGHT)
        send((GATHER, name, s, LEFT), name, src, dst, LEFT)

    def ring_relay(name, s):
        whole = gathered[name]
        arrived((GATHER, name, s, RIGHT), whole.at[rows_of(s), part(left)])
        a = whole.at[pl.ds(s * SEQ, SEQ // 2), part(left)]
        send((GATHER, name, s, X1), name, a, a, RIGHT)
        arrived((GATHER, name, s, LEFT), whole.at[rows_of(s), part(right)])
        b = whole.at[pl.ds(s * SEQ + SEQ // 2, SEQ // 2), part(right)]
        send((GATHER, name, s, X3), name, b, b, LEFT)

    def ring_finish(name, s):
        whole = gathered[name]
        arrived((GATHER, name, s, X1), whole.at[pl.ds(s * SEQ, SEQ // 2), part(across)])
        arrived((GATHER, name, s, X3), whole.at[pl.ds(s * SEQ + SEQ // 2, SEQ // 2), part(across)])

    def sum_start(ph, s, block):
        for slot, (where, n) in enumerate(others):
            r.ys[ph, s, slot] = block(n).astype(bf16)
            send((SUM, ph, s), SUM, r.ys.at[ph, s, slot], r.yr.at[ph, s, slot], where)
        r.own[ph, rows_of(s), :] = block(t)

    def sum_finish(ph, s):
        arrived((SUM, ph, s), r.yr.at[ph, s])

    def summed(ph, s, i, n):
        total = r.own[ph, pl.ds(s * SEQ + i, n), :]
        for slot in range(3):
            total = total + r.yr[ph, s, slot, pl.ds(i, n), :].astype(f32)
        return total

    def totals_start(kind, s, lanes):
        r.rso[kind, s] = row_of(lanes)
        for slot, where in enumerate((RIGHT, LEFT, ACROSS)):
            send((TOTAL, kind, s), TOTAL, r.rso.at[kind, s], r.rsr.at[kind, s, slot], where)

    def totals_finish(kind, s):
        total = r.rso[kind, s]
        arrived((TOTAL, kind, s), r.rsr.at[kind, s])
        for slot in range(3):
            total = total + r.rsr[kind, s, slot]
        r.col[kind, rows_of(s), :] = jnp.transpose(total)[:, 0:1]

    def grad_product(g, lhs, rhs):
        held, width = r.terms[g], COLS[g]

        @pl.loop(0, 4)
        def _(xp):
            a = lhs[:, part(xp)]
            xr = 2 * ((xp // 2 + x // 2) % 2) + (xp + x) % 2
            for first in range(0, width, 256):
                n = min(256, width - first)
                value = tn(a, rhs[:, first : first + n]).astype(bf16)
                for zp in range(4):
                    zr = 2 * ((zp // 2 + z // 2) % 2) + (zp + z) % 2
                    for cp in range(2):
                        mine = (cp + core) % 2
                        at = (zp * 2 + cp) * 32
                        held[mine, 0, 4 * zr + xr, :, first : first + n] = value[at : at + 16]
                        held[mine, 1, 4 * xr + zr, :, first : first + n] = value[at + 16 : at + 32]

        send((GRAD, g, 0), (GRAD, g, 0), held.at[1], r.paired[g], CORE)

    routes = (((Z1, Z2, Z3), (X1, X2, X3)), ((X1, X2, X3), (Z1, Z2, Z3)))

    def grad_first(g):
        held, came = r.terms[g], r.paired[g]
        arrived((GRAD, g, 0), came)

        @pl.loop(0, 16)
        def _(i):
            for half in range(2):
                held[0, half, i] = (held[0, half, i].astype(f32) + came[half, i].astype(f32)).astype(bf16)

        for n in (2, 1, 3):
            for half in range(2):
                send(
                    (GRAD, g, 1),
                    (GRAD, g, 1),
                    held.at[0, half, pl.ds(4 * n, 4)],
                    r.came[g].at[half, pl.ds(4 * n - 4, 4)],
                    routes[half][0][n - 1],
                )

    def grad_second(g):
        held, came = r.terms[g], r.came[g]
        arrived((GRAD, g, 1), came.at[:, pl.ds(0, 12)])

        @pl.loop(0, 4)
        def _(i):
            for half in range(2):
                total = held[0, half, i].astype(f32)
                for n in range(3):
                    total = total + came[half, 4 * n + i].astype(f32)
                held[0, half, i] = total.astype(bf16)

        for n in (2, 1, 3):
            for half in range(2):
                send(
                    (GRAD, g, 2),
                    (GRAD, g, 1),
                    held.at[0, half, pl.ds(n, 1)],
                    came.at[half, pl.ds(11 + n, 1)],
                    routes[half][1][n - 1],
                )

    def grad_last(g):
        held, came = r.terms[g], r.came[g]
        arrived((GRAD, g, 2), came.at[:, pl.ds(12, 3)])
        for half in range(2):
            total = held[0, half, 0].astype(f32)
            for n in range(12, 15):
                total = total + came[half, n].astype(f32)
            rows = pl.ds(half * 16, 16)
            if g == IN:
                for k in range(3):
                    g_in[k, rows, :] = total[:, k * CH : (k + 1) * CH]
            else:
                grads[g][rows, :] = total

    def in_rows(s, step, body):
        @pl.loop(0, SEQ // step)
        def _(n):
            i = pl.multiple_of(n * step, step)
            body(i, pl.ds(pl.multiple_of(s * SEQ + i, step), step))

    barrier = pltpu.get_barrier_semaphore()
    for where in to:
        pl.semaphore_signal(barrier, inc=1, device_id=to[where], device_id_type=MESH)
    fetch(X, x_hbm, r.xg.at[:, part(t)])
    fetch(COT, cot_hbm, r.cg.at[:, part(t)])
    for w in (IN, OUT, GATE, UP, DOWN):
        weight_own(w)
    own_gains = r.gains.at[:, part(t)]
    own_gains[...] = jnp.zeros((8, CH), f32)
    own_gains[0:1, :] = mg[...]
    own_gains[1:2, :] = fg[...]
    pl.semaphore_wait(barrier, len(to))

    weight_cross(IN)
    gather_start(X, x_hbm.at[rows_of(0)], 0)
    for where in (RIGHT, LEFT, ACROSS):
        send(GAINS, GAINS, own_gains, own_gains, where)
    gather_start(X, x_hbm.at[rows_of(1)], 1)
    for w in (OUT, GATE, UP, DOWN):
        weight_cross(w)
    for s in range(2):
        ring_start(COT, cot_hbm.at[rows_of(s)], s)
    weight_around(IN)

    def normalise(s):
        def body(i, rows):
            v = r.xg[rows, :].astype(f32)
            scale = lax.rsqrt(jnp.sum(v * v, axis=1, keepdims=True) / WIDE + EPS)
            r.r1[rows, :] = scale
            r.n1[rows, :] = (v * scale * r.gains[0:1, :]).astype(bf16)

        in_rows(s, 32, body)

    def project(s):
        for k in range(3):
            r.proj[k, rows_of(s), :] = nn(r.n1[rows_of(s), :], r.wi[k])
        mixed = (r.proj[0, rows_of(s), :] * r.proj[2, rows_of(s), :]).astype(bf16)
        r.mpad[s, pl.ds(8, SEQ), :] = mixed.astype(f32)
        r.hs[s] = mixed[SEQ - 16 :]
        send((EDGE, s), EDGE, r.hs.at[s], r.hr.at[s], NEXT)

    local[X].wait()
    arrived(GAINS, r.rsr.at[0, 0])
    gather_finish(X, 0)
    normalise(0)
    weight_share(IN)
    weight_around(OUT)
    weight_ready(IN)
    project(0)
    gather_finish(X, 1)
    normalise(1)
    project(1)
    weight_share(OUT)
    weight_around(GATE)

    def branch(s):
        arrived((EDGE, s), r.hr.at[s])
        edge = r.hr[s].astype(f32)[8:16]
        r.mpad[s, 0:8, :] = jnp.where(ctx > 0, edge, 0.0)

        for i in range(0, SEQ, 64):
            rows = pl.ds(s * SEQ + i, 64)
            c = (
                taps[0:1, :] * r.mpad[s, i + 6 : i + 70, :]
                + taps[1:2, :] * r.mpad[s, i + 7 : i + 71, :]
                + taps[2:3, :] * r.mpad[s, i + 8 : i + 72, :]
            )
            r.conv[rows, :] = c
            r.gated[rows, :] = (r.proj[1, rows, :] * c).astype(bf16)

        sum_start(0, s, lambda n: nn(r.gated[rows_of(s), :], r.wo[:, part(n)]))

    weight_ready(OUT)
    branch(0)
    branch(1)
    ring_relay(COT, 0)
    ring_relay(COT, 1)
    weight_around(UP)
    weight_share(GATE)

    def second(s):
        sum_finish(0, s)

        def body(i, rows):
            value = r.xg[rows, part(t)].astype(f32) + summed(0, s, i, 32)
            r.resid[rows, :] = value
            r.qg[rows, part(t)] = (value * fg[...]).astype(bf16)

        in_rows(s, 32, body)
        gather_start(Q, r.qg.at[rows_of(s), part(t)], s)

    second(0)
    second(1)
    weight_around(DOWN)
    weight_share(UP)
    local[COT].wait()

    def feed(s):
        gather_finish(Q, s)

        def scales(i, rows):
            v = r.qg[rows, :].astype(f32) * (1.0 / r.gains[1:2, :])
            r.r2[rows, :] = lax.rsqrt(jnp.sum(v * v, axis=1, keepdims=True) / WIDE + EPS)

        in_rows(s, 32, scales)
        if s == 0:
            weight_ready(GATE)
        q = r.qg[rows_of(s), :]
        slices = [pl.ds(first, min(256, HID - first)) for first in range(0, HID, 256)]
        for cols in slices:
            r.tg[:, cols] = nn(q, r.wg[:, cols])
        if s == 0:
            weight_share(DOWN)
            weight_ready(UP)
        for cols in slices:
            r.tu[:, cols] = nn(q, r.wu[:, cols])
        ring_finish(COT, s)
        if s == 0:
            weight_ready(DOWN)
        c = r.cg[rows_of(s), :]
        for cols in slices:
            r.td[:, cols] = nt(c, r.wd[cols, :])

        def body(i, rows):
            here = pl.ds(i, 16)
            scale = r.r2[rows, :]
            total = jnp.zeros((16, 128), f32)
            for first in range(0, HID, 384):
                cols = pl.ds(first, 384)
                gate, up, dh = r.tg[here, cols] * scale, r.tu[here, cols] * scale, r.td[here, cols]
                sg = jax.nn.sigmoid(gate)
                act = gate * sg
                r.hid[rows, cols] = (act * up).astype(bf16)
                d_gate = dh * up * sg * (1.0 + gate * (1.0 - sg))
                d_up = dh * act
                r.eg[rows, cols] = (d_gate * scale).astype(bf16)
                r.eu[rows, cols] = (d_up * scale).astype(bf16)
                both = d_gate * gate + d_up * up
                for j in range(0, 384, 128):
                    total = total + both[:, j : j + 128]
            r.lanes[here, :] = total

        in_rows(s, 16, body)
        sum_start(
            1,
            s,
            lambda n: nt(r.eg[rows_of(s), :], r.wg[part(n), :]) + nt(r.eu[rows_of(s), :], r.wu[part(n), :]),
        )
        totals_start(0, s, r.lanes[...])

    feed(0)
    feed(1)

    small = r.sums.at[0]
    small[...] = jnp.zeros((8, CH), f32)

    def through_norm(s):
        sum_finish(1, s)
        totals_finish(0, s)

        def body(i, rows):
            g = summed(1, s, i, 32)
            value, scale = r.resid[rows, :], r.r2[rows, :]
            small[1:2, :] += jnp.sum(g * value, axis=0, keepdims=True)
            d = (
                r.cg[rows, part(t)].astype(f32)
                + fg[...] * g
                - value * (scale * scale * r.col[0, rows, :] * (1.0 / WIDE))
            )
            r.dres[rows, :] = d
            r.bg[rows, part(t)] = d.astype(bf16)

        in_rows(s, 32, body)
        gather_start(B, r.bg.at[rows_of(s), part(t)], s)

    through_norm(0)
    grad_product(GATE, r.qg, r.eg)
    grad_product(UP, r.qg, r.eu)
    through_norm(1)

    def deliver(s):
        sum_start(2, s, lambda n: nn(r.hid[rows_of(s), :], r.wd[:, part(n)]))

    deliver(0)
    grad_first(GATE)

    def back(s):
        gather_finish(B, s)
        d = nt(r.bg[rows_of(s), :], r.wo[...])
        r.tg[:, 0:CH] = d
        for i in range(0, SEQ, 64):
            rows = pl.ds(s * SEQ + i, 64)
            d = r.tg[i : i + 64, 0:CH]
            d_conv = d * r.proj[1, rows, :]
            r.dpad[s, i : i + 64, :] = d_conv
            d_c = d * r.conv[rows, :]
            r.dproj[rows, CH : 2 * CH] = d_c.astype(bf16)
            for j in range(3):
                small[2 + j : 3 + j, :] += jnp.sum(
                    d_conv * r.mpad[s, i + 6 + j : i + 70 + j, :], axis=0, keepdims=True
                )
        r.ds[s] = r.dpad[s, 0:8, :]
        send((BACK, s), BACK, r.ds.at[s], r.dr.at[s], PREV)

    def mixer(s):
        arrived((BACK, s), r.dr.at[s])
        r.dpad[s, SEQ : SEQ + 8, :] = jnp.where(ctx < 15, r.dr[s], 0.0)
        for i in range(0, SEQ, 64):
            rows = pl.ds(s * SEQ + i, 64)
            d_mixed = (
                taps[2:3, :] * r.dpad[s, i : i + 64, :]
                + taps[1:2, :] * r.dpad[s, i + 1 : i + 65, :]
                + taps[0:1, :] * r.dpad[s, i + 2 : i + 66, :]
            )
            b, c, xi = r.proj[0, rows, :], r.proj[1, rows, :], r.proj[2, rows, :]
            d_b, d_x = (d_mixed * xi).astype(bf16), (d_mixed * b).astype(bf16)
            r.dproj[rows, 0:CH] = d_b
            r.dproj[rows, 2 * CH :] = d_x
            d_c = r.dproj[rows, CH : 2 * CH].astype(f32)
            both = d_b.astype(f32) * b + d_x.astype(f32) * xi + d_c * c
            r.lanes[i : i + 64, :] = both[:, 0:128] + both[:, 128:256]

        def term(n):
            total = nt(r.dproj[rows_of(s), 0:CH], r.wi[0, part(n), :])
            for k in (1, 2):
                total += nt(r.dproj[rows_of(s), k * CH : (k + 1) * CH], r.wi[k, part(n), :])
            return total

        sum_start(3, s, term)
        totals_start(1, s, r.lanes[...])

    back(0)
    grad_product(DOWN, r.cg, r.hid)
    grad_first(UP)
    mixer(0)
    back(1)
    grad_product(OUT, r.bg, r.gated)
    grad_second(GATE)
    grad_first(DOWN)
    mixer(1)
    grad_product(IN, r.n1, r.dproj)
    deliver(1)
    grad_second(UP)
    grad_first(OUT)

    def finish(s):
        sum_finish(3, s)
        totals_finish(1, s)

        def body(i, rows):
            g = summed(3, s, i, 32)
            value, scale = r.xg[rows, part(t)].astype(f32), r.r1[rows, :]
            small[0:1, :] += jnp.sum(g * (value * scale), axis=0, keepdims=True)
            input_grad[rows, :] = (
                r.dres[rows, :]
                + scale * (mg[...] * g)
                - value * (scale * scale * r.col[1, rows, :] * (1.0 / WIDE))
            )

        in_rows(s, 32, body)

    finish(0)
    grad_first(IN)
    grad_second(DOWN)
    grad_last(GATE)
    finish(1)
    for n, where in enumerate((CORE, Z1, Z2, Z3, Z1C, Z2C, Z3C)):
        send((SMALL, 0), SMALL, r.sums.at[0], r.sumr.at[n], where)
    grad_second(OUT)
    grad_last(UP)
    for s in range(2):
        sum_finish(2, s)

        def body(i, rows):
            block_out[rows, :] = (r.resid[rows, :] + summed(2, s, i, 32)).astype(bf16)

        in_rows(s, 32, body)
    total = r.sums[0]
    arrived((SMALL, 0), r.sumr.at[pl.ds(0, 7)])
    for n in range(7):
        total = total + r.sumr[n]
    r.sums[1] = total
    for n, where in enumerate((X1, X2, X3)):
        send((SMALL, 1), SMALL, r.sums.at[1], r.sumr.at[7 + n], where)
    grad_second(IN)
    grad_last(DOWN)
    grad_last(OUT)
    arrived((SMALL, 1), r.sumr.at[pl.ds(7, 3)])
    for n in range(7, 10):
        total = total + r.sumr[n]
    g_small[...] = total
    grad_last(IN)

    left_all(SUM, r.ys)
    left_all(GATHER, r.ys.at[pl.ds(0, 3)])
    left_all(COT, r.ys.at[0])
    left_all(TOTAL, r.rsr)
    left_all(GAINS, r.rsr.at[0, 0])
    left_all(SMALL, r.sumr)
    left_all(EDGE, r.hr)
    left_all(BACK, r.dr)
    for w in (IN, OUT, GATE, UP, DOWN):
        left_all((AHEAD, w), piece(w, 0, 0, weights[w][2]))
        left_all((GRAD, w, 0), r.paired[w])
        left_all((GRAD, w, 1), r.came[w])


def deliver_kernel(*refs):
    small, whole = refs[0], refs[1:8]
    ends, sums = refs[8:15], refs[15:18]
    held, sem = refs[18:25], refs[25]
    taken = [pltpu.make_async_copy(a, b, sem.at[0, n]) for n, (a, b) in enumerate(zip(whole, held))]
    copies = [pltpu.make_async_copy(a, b, sem.at[1, n]) for n, (a, b) in enumerate(zip(held, ends))]
    for copy in taken:
        copy.start()
    for first, then in zip(taken, copies):
        first.wait()
        then.start()
    sums[0][...] = small[0]
    sums[1][...] = small[1]
    sums[2][...] = small[2:5]
    for copy in copies:
        copy.wait()


def on_device(block_input, in_proj, out_proj, gate_proj, up_proj, down_proj, mixer_gain, ffn_gain, conv_kernel, cotangent):
    shapes = scratch()

    def kernel(*refs):
        taken, held = refs[18:], {}
        count = 0
        for name, shape in shapes.items():
            if isinstance(shape, list):
                held[name] = taken[count : count + len(shape)]
                count += len(shape)
            else:
                held[name] = taken[count]
                count += 1
        block_kernel(types.SimpleNamespace(**held), *refs[:18])

    hbm, vmem = pl.BlockSpec(memory_space=pl.ANY), pl.BlockSpec(memory_space=pltpu.VMEM)
    out = jax.ShapeDtypeStruct
    *whole, small = pl.pallas_call(
        kernel,
        out_shape=(
            out((TOK, CH), bf16),
            out((TOK, CH), f32),
            out((3, 32, CH), f32),
            out((32, CH), f32),
            out((32, HID), f32),
            out((32, HID), f32),
            out((32, HID), f32),
            out((8, CH), f32),
        ),
        in_specs=[hbm] * 7 + [vmem] * 3,
        out_specs=[vmem] * 8,
        scratch_shapes=jax.tree.leaves(list(shapes.values())),
        compiler_params=pltpu.CompilerParams(
            collective_id=0, has_side_effects=True, vmem_limit_bytes=62 * 1024 * 1024
        ),
    )(
        block_input.reshape(TOK, CH),
        cotangent.reshape(TOK, CH),
        jnp.transpose(in_proj, (1, 0, 2)),
        out_proj,
        gate_proj,
        up_proj,
        down_proj,
        mixer_gain.reshape(1, CH),
        ffn_gain.reshape(1, CH),
        conv_kernel,
    )
    block_out, input_grad, g_in, g_out, g_gate, g_up, g_down, mixer_sum, ffn_sum, taps_sum = pl.pallas_call(
        deliver_kernel,
        out_shape=(
            *(out(a.shape, a.dtype) for a in whole),
            out((CH,), f32),
            out((CH,), f32),
            out((3, CH), f32),
        ),
        in_specs=[vmem] + [hbm] * 7,
        out_specs=[hbm] * 7 + [vmem] * 3,
        scratch_shapes=[pltpu.VMEM(a.shape, a.dtype) for a in whole] + [pltpu.SemaphoreType.DMA((2, 7))],
    )(small, *whole)
    return (
        block_out.reshape(2, SEQ, CH),
        input_grad.reshape(2, SEQ, CH),
        jnp.transpose(g_in, (1, 0, 2)),
        g_out.T,
        g_gate,
        g_up,
        g_down.T,
        mixer_sum,
        ffn_sum,
        taps_sum,
    )


def solution(mesh):
    return jax.shard_map(
        on_device,
        mesh=mesh,
        in_specs=(
            P("shard", "ctx", "tp"),
            P("shard", None, "tp"),
            P("tp", "shard"),
            P("shard", "tp"),
            P("shard", "tp"),
            P("tp", "shard"),
            P("tp"),
            P("tp"),
            P(None, "tp"),
            P("shard", "ctx", "tp"),
        ),
        out_specs=(
            P("shard", "ctx", "tp"),
            P("shard", "ctx", "tp"),
            P(("shard", "ctx"), None, "tp"),
            P("tp", ("shard", "ctx")),
            P(("shard", "ctx"), "tp"),
            P(("shard", "ctx"), "tp"),
            P("tp", ("shard", "ctx")),
            P("tp"),
            P("tp"),
            P(None, "tp"),
        ),
        check_vma=False,
    )
```

```python
import types

import jax
import jax.numpy as jnp
from jax import lax
from jax.experimental import pallas as pl
from jax.experimental.pallas import tpu as pltpu
from jax.sharding import PartitionSpec as P

EPS = 1e-05
MESH = pl.DeviceIdType.MESH
f32, bf16 = jnp.float32, jnp.bfloat16
WIDE, SEQ, TOK, CH, HID = 1024, 256, 512, 256, 1152
DOWN, GATE, UP, OUT, IN = range(5)
COLS = (HID, HID, HID, CH, 3 * CH)
RIGHT, LEFT, ACROSS, CORE, Z1, X1, Z3, X3, NEXT, PREV, X2, Z2, Z1C, Z2C, Z3C = range(15)
AHEAD, GATHER, SUM, TOTAL, GRAD, GAINS, EDGE, BACK, SMALL = range(9)
X, COT, Q, B = range(20, 24)
RING_GATHERS, RING_SUMS = (X, COT), ()
def scratch():
    v = pltpu.VMEM
    shapes = dict(
        xg=v((TOK, WIDE), bf16),
        cg=v((TOK, WIDE), bf16),
        qg=v((TOK, WIDE), bf16),
        bg=v((TOK, WIDE), bf16),
        n1=v((TOK, WIDE), bf16),
        gains=v((8, WIDE), f32),
        r1=v((TOK, 1), f32),
        r2=v((TOK, 1), f32),
        col=v((2, TOK, 1), f32),
        wi=v((3, WIDE, CH), bf16),
        wo=v((CH, WIDE), bf16),
        wg=v((WIDE, HID), bf16),
        wu=v((WIDE, HID), bf16),
        wd=v((HID, WIDE), bf16),
        proj=v((3, TOK, CH), f32),
        mpad=v((2, SEQ + 8, CH), f32),
        hs=v((2, 16, CH), bf16),
        hr=v((2, 16, CH), bf16),
        conv=v((TOK, CH), f32),
        gated=v((TOK, CH), bf16),
        ys=v((4, 2, 3, SEQ, CH), bf16),
        yr=v((4, 2, 3, SEQ, CH), bf16),
        yo=v((4, 2, 2, SEQ // 2, CH), bf16),
        own=v((4, TOK, CH), f32),
        resid=v((TOK, CH), f32),
        tg=v((SEQ, HID), f32),
        tu=v((SEQ, HID), f32),
        td=v((SEQ, HID), f32),
        lanes=v((SEQ, 128), f32),
        hid=v((TOK, HID), bf16),
        eg=v((TOK, HID), bf16),
        eu=v((TOK, HID), bf16),
        dres=v((TOK, CH), f32),
        dpad=v((2, SEQ + 8, CH), f32),
        ds=v((2, 8, CH), f32),
        dr=v((2, 8, CH), f32),
        dproj=v((TOK, 3 * CH), bf16),
        rso=v((2, 2, 8, SEQ), f32),
        rsr=v((2, 2, 3, 8, SEQ), f32),
        sums=v((2, 8, CH), f32),
        sumr=v((10, 8, CH), f32),
        terms=[v((2, 2, 16, 16, n), bf16) for n in COLS],
        paired=[v((2, 16, 16, n), bf16) for n in COLS],
        came=[v((2, 15, 16, n), bf16) for n in COLS],
        ssem=pltpu.SemaphoreType.DMA((28,)),
        rsem=pltpu.SemaphoreType.DMA((65,)),
        lsem=pltpu.SemaphoreType.DMA((7,)),
    )
    return shapes


def nn(a, b):
    return jnp.dot(a, b, preferred_element_type=f32)


def nt(a, b):
    return lax.dot_general(a, b, (((1,), (1,)), ((), ())), preferred_element_type=f32)


def tn(a, b):
    return lax.dot_general(a, b, (((0,), (0,)), ((), ())), preferred_element_type=f32)


def row_of(lanes):
    ones = jnp.ones((8, lanes.shape[1]), f32)
    return lax.dot_general(
        ones, lanes, (((1,), (1,)), ((), ())), precision=lax.Precision.HIGHEST, preferred_element_type=f32
    )


def block_kernel(r, *refs):
    (x_hbm, cot_hbm, in_hbm, out_hbm, gate_hbm, up_hbm, down_hbm, mg, fg, taps) = refs[:10]
    (block_out, input_grad, g_in, g_out, g_gate, g_up, g_down, g_small) = refs[10:]
    grads = {DOWN: g_down, GATE: g_gate, UP: g_up, OUT: g_out, IN: g_in}
    ssem, rsem, lsem = r.ssem, r.rsem, r.lsem

    shard, ctx, t = lax.axis_index("shard"), lax.axis_index("ctx"), lax.axis_index("tp")
    core, z, x = ctx % 2, (ctx // 2) % 4, shard * 2 + ctx // 8

    def dev(xx, zz, cc, tt):
        return (xx // 2, (xx % 2) * 8 + zz * 2 + cc, tt)

    z1, z3, x1, x3 = z + 1 - 2 * (z % 2), 3 - z, x + 1 - 2 * (x % 2), 3 - x
    right, left, across = (t + 1) % 4, (t + 3) % 4, (t + 2) % 4
    to = {
        RIGHT: (shard, ctx, right),
        LEFT: (shard, ctx, left),
        ACROSS: (shard, ctx, across),
        CORE: dev(x, z, 1 - core, t),
        Z1: dev(x, z1, core, t),
        Z3: dev(x, z3, core, t),
        X1: dev(x1, z, core, t),
        X3: dev(x3, z, core, t),
        NEXT: (shard, (ctx + 1) % 16, t),
        PREV: (shard, (ctx + 15) % 16, t),
        X2: dev((x + 2) % 4, z, core, t),
        Z2: dev(x, (z + 2) % 4, core, t),
        Z1C: dev(x, z1, 1 - core, t),
        Z2C: dev(x, (z + 2) % 4, 1 - core, t),
        Z3C: dev(x, z3, 1 - core, t),
    }

    came_ids, sent_ids, local = {}, {}, {}
    gathered = {X: r.xg, COT: r.cg, Q: r.qg, B: r.bg}

    def send(key, group, src, dst, where):
        n, m = came_ids.setdefault(key, len(came_ids)), sent_ids.setdefault(group, len(sent_ids))
        pltpu.make_async_remote_copy(
            src_ref=src,
            dst_ref=dst,
            send_sem=ssem.at[m],
            recv_sem=rsem.at[n],
            device_id=to[where],
            device_id_type=MESH,
        ).start()

    def arrived(key, size):
        pltpu.make_async_copy(size, size, rsem.at[came_ids[key]]).wait()

    def left_all(group, size):
        pltpu.make_async_copy(size, size, ssem.at[sent_ids[group]]).wait()

    def fetch(key, src, dst):
        copy = pltpu.make_async_copy(src, dst, lsem.at[len(local)])
        copy.start()
        local[key] = copy

    def part(n):
        return pl.ds(pl.multiple_of(n * CH, CH), CH)

    def rows_of(s):
        return pl.ds(s * SEQ, SEQ)

    weights = {
        IN: (in_hbm, r.wi, 512),
        OUT: (out_hbm, r.wo, 256),
        GATE: (gate_hbm, r.wg, 512),
        UP: (up_hbm, r.wu, 512),
        DOWN: (down_hbm, r.wd, HID),
    }

    def piece(w, half, first, count):
        whole = weights[w][1]
        if w == IN:
            return whole.at[:, pl.ds(pl.multiple_of(half * 512 + first, 32), count), :]
        if w in (GATE, UP):
            return whole.at[pl.ds(pl.multiple_of(half * 512 + first, 32), count), :]
        return whole.at[pl.ds(pl.multiple_of(first, 16), count), pl.ds(pl.multiple_of(half * 512, 512), 512)]

    def source(w, first, count):
        held = weights[w][0]
        at = pl.ds(pl.multiple_of(first, 16), count)
        return held.at[:, at, :] if w == IN else held.at[at, :]

    def quarter(w):
        return weights[w][2] // 4

    pair = z % 2

    def weight_own(w):
        fetch(w, weights[w][0], piece(w, shard, 0, weights[w][2]))

    def weight_cross(w):
        n = quarter(w)
        first = (pair * 2 + core) * n
        send((AHEAD, w, 0), (AHEAD, w), source(w, first, n), piece(w, shard, first, n), X3)

    def weight_around(w):
        n = quarter(w)
        first = (pair * 2 + core) * n
        mine = piece(w, 1 - shard, first, n)
        arrived((AHEAD, w, 0), mine)
        a, b = piece(w, 1 - shard, first, n // 2), piece(w, 1 - shard, first + n // 2, n // 2)
        send((AHEAD, w, 1), (AHEAD, w), a, a, Z1)
        send((AHEAD, w, 1), (AHEAD, w), b, b, Z3)
        send((AHEAD, w, 2), (AHEAD, w), mine, mine, CORE)

    def weight_share(w):
        n = quarter(w)
        first = ((1 - pair) * 2 + core) * n
        other = piece(w, 1 - shard, first, n)
        arrived((AHEAD, w, 1), other)
        send((AHEAD, w, 2), (AHEAD, w), other, other, CORE)

    def weight_ready(w):
        arrived((AHEAD, w, 2), piece(w, 1 - shard, 0, 2 * quarter(w)))
        local[w].wait()

    def gather_start(name, src, s):
        half = SEQ // 2

        def go(key, first, where, count=half):
            dst = gathered[name].at[pl.ds(s * SEQ + first, count), part(t)]
            send((GATHER, name, s, key), (GATHER, name), src.at[pl.ds(first, count)], dst, where)

        if name not in RING_GATHERS:
            for where in (RIGHT, LEFT, ACROSS):
                go(ACROSS, 0, where, SEQ)
            return
        go(RIGHT, 0, RIGHT)
        go(LEFT, half, LEFT)
        go(ACROSS, half, RIGHT)
        go(ACROSS, 0, LEFT)

    def gather_relay(name, s):
        if name not in RING_GATHERS:
            return
        half, whole = SEQ // 2, gathered[name]
        a = whole.at[pl.ds(s * SEQ, half), part(left)]
        arrived((GATHER, name, s, RIGHT), a)
        send((GATHER, name, s, ACROSS), (GATHER, name), a, a, RIGHT)
        b = whole.at[pl.ds(s * SEQ + half, half), part(right)]
        arrived((GATHER, name, s, LEFT), b)
        send((GATHER, name, s, ACROSS), (GATHER, name), b, b, LEFT)

    def gather_finish(name, s):
        arrived((GATHER, name, s, ACROSS), r.ys.at[0, 0, pl.ds(0, 2 if name in RING_GATHERS else 3)])

    top, low = pl.ds(0, SEQ // 2), pl.ds(SEQ // 2, SEQ // 2)

    def sum_start(ph, s, block):
        ys, yr, yo = r.ys.at[ph, s], r.yr.at[ph, s], r.yo.at[ph, s]
        if ph not in RING_SUMS:
            for slot, (where, n) in enumerate(((RIGHT, right), (LEFT, left), (ACROSS, across))):
                ys[slot] = block(n).astype(bf16)
                send((SUM, ph, s, ACROSS), (SUM, ph), ys.at[slot], yr.at[slot], where)
            r.own[ph, rows_of(s), :] = block(t)
            return
        ys[2] = block(across).astype(bf16)
        send((SUM, ph, s, RIGHT), (SUM, ph), ys.at[2, top], yo.at[0], RIGHT)
        send((SUM, ph, s, LEFT), (SUM, ph), ys.at[2, low], yo.at[1], LEFT)
        ys[0] = block(right).astype(bf16)
        send((SUM, ph, s, ACROSS), (SUM, ph), ys.at[0, low], yr.at[0, low], RIGHT)
        ys[1] = block(left).astype(bf16)
        send((SUM, ph, s, ACROSS), (SUM, ph), ys.at[1, top], yr.at[1, top], LEFT)
        r.own[ph, rows_of(s), :] = block(t)

    def sum_relay(ph, s):
        if ph not in RING_SUMS:
            return
        ys, yr, yo = r.ys.at[ph, s], r.yr.at[ph, s], r.yo.at[ph, s]
        arrived((SUM, ph, s, RIGHT), yo.at[0])
        ys[0, top, :] = (ys[0, top, :].astype(f32) + yo[0].astype(f32)).astype(bf16)
        send((SUM, ph, s, ACROSS), (SUM, ph), ys.at[0, top], yr.at[0, top], RIGHT)
        arrived((SUM, ph, s, LEFT), yo.at[1])
        ys[1, low, :] = (ys[1, low, :].astype(f32) + yo[1].astype(f32)).astype(bf16)
        send((SUM, ph, s, ACROSS), (SUM, ph), ys.at[1, low], yr.at[1, low], LEFT)

    def sum_finish(ph, s):
        arrived((SUM, ph, s, ACROSS), r.yr.at[ph, s, pl.ds(0, 2 if ph in RING_SUMS else 3)])

    def summed(ph, s, i, n):
        total = r.own[ph, pl.ds(s * SEQ + i, n), :]
        for slot in range(2 if ph in RING_SUMS else 3):
            total = total + r.yr[ph, s, slot, pl.ds(i, n), :].astype(f32)
        return total

    def totals_start(kind, s, lanes):
        r.rso[kind, s] = row_of(lanes)
        for slot, where in enumerate((RIGHT, LEFT, ACROSS)):
            send((TOTAL, kind, s), TOTAL, r.rso.at[kind, s], r.rsr.at[kind, s, slot], where)

    def totals_finish(kind, s):
        total = r.rso[kind, s]
        arrived((TOTAL, kind, s), r.rsr.at[kind, s])
        for slot in range(3):
            total = total + r.rsr[kind, s, slot]
        r.col[kind, rows_of(s), :] = jnp.transpose(total)[:, 0:1]

    def grad_product(g, lhs, rhs):
        held, width = r.terms[g], COLS[g]

        @pl.loop(0, 4)
        def _(xp):
            a = lhs[:, part(xp)]
            xr = 2 * ((xp // 2 + x // 2) % 2) + (xp + x) % 2
            for first in range(0, width, 256):
                n = min(256, width - first)
                value = tn(a, rhs[:, first : first + n]).astype(bf16)
                for zp in range(4):
                    zr = 2 * ((zp // 2 + z // 2) % 2) + (zp + z) % 2
                    for cp in range(2):
                        mine = (cp + core) % 2
                        at = (zp * 2 + cp) * 32
                        held[mine, 0, 4 * zr + xr, :, first : first + n] = value[at : at + 16]
                        held[mine, 1, 4 * xr + zr, :, first : first + n] = value[at + 16 : at + 32]

        send((GRAD, g, 0), (GRAD, g, 0), held.at[1], r.paired[g], CORE)

    routes = (((Z1, Z2, Z3), (X1, X2, X3)), ((X1, X2, X3), (Z1, Z2, Z3)))

    def grad_first(g):
        held, came = r.terms[g], r.paired[g]
        arrived((GRAD, g, 0), came)

        @pl.loop(0, 16)
        def _(i):
            for half in range(2):
                held[0, half, i] = (held[0, half, i].astype(f32) + came[half, i].astype(f32)).astype(bf16)

        for n in (2, 1, 3):
            for half in range(2):
                send(
                    (GRAD, g, 1),
                    (GRAD, g, 1),
                    held.at[0, half, pl.ds(4 * n, 4)],
                    r.came[g].at[half, pl.ds(4 * n - 4, 4)],
                    routes[half][0][n - 1],
                )

    def grad_second(g):
        held, came = r.terms[g], r.came[g]
        arrived((GRAD, g, 1), came.at[:, pl.ds(0, 12)])

        @pl.loop(0, 4)
        def _(i):
            for half in range(2):
                total = held[0, half, i].astype(f32)
                for n in range(3):
                    total = total + came[half, 4 * n + i].astype(f32)
                held[0, half, i] = total.astype(bf16)

        for n in (2, 1, 3):
            for half in range(2):
                send(
                    (GRAD, g, 2),
                    (GRAD, g, 1),
                    held.at[0, half, pl.ds(n, 1)],
                    came.at[half, pl.ds(11 + n, 1)],
                    routes[half][1][n - 1],
                )

    def grad_last(g):
        held, came = r.terms[g], r.came[g]
        arrived((GRAD, g, 2), came.at[:, pl.ds(12, 3)])
        for half in range(2):
            total = held[0, half, 0].astype(f32)
            for n in range(12, 15):
                total = total + came[half, n].astype(f32)
            rows = pl.ds(half * 16, 16)
            if g == IN:
                for k in range(3):
                    g_in[k, rows, :] = total[:, k * CH : (k + 1) * CH]
            else:
                grads[g][rows, :] = total

    def in_rows(s, step, body):
        @pl.loop(0, SEQ // step)
        def _(n):
            i = pl.multiple_of(n * step, step)
            body(i, pl.ds(pl.multiple_of(s * SEQ + i, step), step))

    barrier = pltpu.get_barrier_semaphore()
    for where in to:
        pl.semaphore_signal(barrier, inc=1, device_id=to[where], device_id_type=MESH)
    fetch(X, x_hbm, r.xg.at[:, part(t)])
    fetch(COT, cot_hbm, r.cg.at[:, part(t)])
    for w in (IN, OUT, GATE, UP, DOWN):
        weight_own(w)
    own_gains = r.gains.at[:, part(t)]
    own_gains[...] = jnp.zeros((8, CH), f32)
    own_gains[0:1, :] = mg[...]
    own_gains[1:2, :] = fg[...]
    pl.semaphore_wait(barrier, len(to))

    weight_cross(IN)
    gather_start(X, x_hbm.at[rows_of(0)], 0)
    for where in (RIGHT, LEFT, ACROSS):
        send(GAINS, GAINS, own_gains, own_gains, where)
    gather_start(X, x_hbm.at[rows_of(1)], 1)
    for w in (OUT, GATE, UP, DOWN):
        weight_cross(w)
    for s in range(2):
        gather_relay(X, s)
    for s in range(2):
        gather_start(COT, cot_hbm.at[rows_of(s)], s)
    weight_around(IN)

    def normalise(s):
        def body(i, rows):
            v = r.xg[rows, :].astype(f32)
            scale = lax.rsqrt(jnp.sum(v * v, axis=1, keepdims=True) / WIDE + EPS)
            r.r1[rows, :] = scale
            r.n1[rows, :] = (v * scale * r.gains[0:1, :]).astype(bf16)

        in_rows(s, 32, body)

    def project(s):
        for k in range(3):
            r.proj[k, rows_of(s), :] = nn(r.n1[rows_of(s), :], r.wi[k])
        mixed = (r.proj[0, rows_of(s), :] * r.proj[2, rows_of(s), :]).astype(bf16)
        r.mpad[s, pl.ds(8, SEQ), :] = mixed.astype(f32)
        r.hs[s] = mixed[SEQ - 16 :]
        send((EDGE, s), EDGE, r.hs.at[s], r.hr.at[s], NEXT)

    local[X].wait()
    arrived(GAINS, r.rsr.at[0, 0])
    gather_finish(X, 0)
    normalise(0)
    weight_share(IN)
    weight_around(OUT)
    weight_ready(IN)
    project(0)
    gather_finish(X, 1)
    normalise(1)
    project(1)
    weight_share(OUT)
    gather_relay(COT, 0)
    gather_relay(COT, 1)
    weight_around(GATE)

    def branch(s):
        arrived((EDGE, s), r.hr.at[s])
        edge = r.hr[s].astype(f32)[8:16]
        r.mpad[s, 0:8, :] = jnp.where(ctx > 0, edge, 0.0)

        for i in range(0, SEQ, 64):
            rows = pl.ds(s * SEQ + i, 64)
            c = (
                taps[0:1, :] * r.mpad[s, i + 6 : i + 70, :]
                + taps[1:2, :] * r.mpad[s, i + 7 : i + 71, :]
                + taps[2:3, :] * r.mpad[s, i + 8 : i + 72, :]
            )
            r.conv[rows, :] = c
            r.gated[rows, :] = (r.proj[1, rows, :] * c).astype(bf16)

        sum_start(0, s, lambda n: nn(r.gated[rows_of(s), :], r.wo[:, part(n)]))

    weight_ready(OUT)
    branch(0)
    branch(1)
    weight_around(UP)
    weight_share(GATE)
    sum_relay(0, 0)
    sum_relay(0, 1)

    def second(s):
        sum_finish(0, s)

        def body(i, rows):
            value = r.xg[rows, part(t)].astype(f32) + summed(0, s, i, 32)
            r.resid[rows, :] = value
            r.qg[rows, part(t)] = (value * fg[...]).astype(bf16)

        in_rows(s, 32, body)
        gather_start(Q, r.qg.at[rows_of(s), part(t)], s)

    second(0)
    second(1)
    weight_around(DOWN)
    weight_share(UP)
    local[COT].wait()
    gather_relay(Q, 0)
    gather_relay(Q, 1)

    def feed(s):
        gather_finish(Q, s)

        def scales(i, rows):
            v = r.qg[rows, :].astype(f32) * (1.0 / r.gains[1:2, :])
            r.r2[rows, :] = lax.rsqrt(jnp.sum(v * v, axis=1, keepdims=True) / WIDE + EPS)

        in_rows(s, 32, scales)
        if s == 0:
            weight_ready(GATE)
        q = r.qg[rows_of(s), :]
        slices = [pl.ds(first, min(256, HID - first)) for first in range(0, HID, 256)]
        for cols in slices:
            r.tg[:, cols] = nn(q, r.wg[:, cols])
        if s == 0:
            weight_share(DOWN)
            weight_ready(UP)
        for cols in slices:
            r.tu[:, cols] = nn(q, r.wu[:, cols])
        gather_finish(COT, s)
        if s == 0:
            weight_ready(DOWN)
        c = r.cg[rows_of(s), :]
        for cols in slices:
            r.td[:, cols] = nt(c, r.wd[cols, :])
        if s == 1:
            sum_relay(1, 0)

        def body(i, rows):
            here = pl.ds(i, 16)
            scale = r.r2[rows, :]
            total = jnp.zeros((16, 128), f32)
            for first in range(0, HID, 384):
                cols = pl.ds(first, 384)
                gate, up, dh = r.tg[here, cols] * scale, r.tu[here, cols] * scale, r.td[here, cols]
                sg = jax.nn.sigmoid(gate)
                act = gate * sg
                r.hid[rows, cols] = (act * up).astype(bf16)
                d_gate = dh * up * sg * (1.0 + gate * (1.0 - sg))
                d_up = dh * act
                r.eg[rows, cols] = (d_gate * scale).astype(bf16)
                r.eu[rows, cols] = (d_up * scale).astype(bf16)
                both = d_gate * gate + d_up * up
                for j in range(0, 384, 128):
                    total = total + both[:, j : j + 128]
            r.lanes[here, :] = total

        in_rows(s, 16, body)
        sum_start(
            1,
            s,
            lambda n: nt(r.eg[rows_of(s), :], r.wg[part(n), :]) + nt(r.eu[rows_of(s), :], r.wu[part(n), :]),
        )
        totals_start(0, s, r.lanes[...])

    feed(0)
    feed(1)

    small = r.sums.at[0]
    small[...] = jnp.zeros((8, CH), f32)

    def through_norm(s):
        sum_finish(1, s)
        totals_finish(0, s)

        def body(i, rows):
            g = summed(1, s, i, 32)
            value, scale = r.resid[rows, :], r.r2[rows, :]
            small[1:2, :] += jnp.sum(g * value, axis=0, keepdims=True)
            d = (
                r.cg[rows, part(t)].astype(f32)
                + fg[...] * g
                - value * (scale * scale * r.col[0, rows, :] * (1.0 / WIDE))
            )
            r.dres[rows, :] = d
            r.bg[rows, part(t)] = d.astype(bf16)

        in_rows(s, 32, body)
        gather_start(B, r.bg.at[rows_of(s), part(t)], s)

    through_norm(0)
    grad_product(GATE, r.qg, r.eg)
    sum_relay(1, 1)
    gather_relay(B, 0)
    grad_product(UP, r.qg, r.eu)
    through_norm(1)

    def deliver(s):
        sum_start(2, s, lambda n: nn(r.hid[rows_of(s), :], r.wd[:, part(n)]))

    deliver(0)
    grad_first(GATE)

    def back(s):
        gather_finish(B, s)
        d = nt(r.bg[rows_of(s), :], r.wo[...])
        r.tg[:, 0:CH] = d
        for i in range(0, SEQ, 64):
            rows = pl.ds(s * SEQ + i, 64)
            d = r.tg[i : i + 64, 0:CH]
            d_conv = d * r.proj[1, rows, :]
            r.dpad[s, i : i + 64, :] = d_conv
            d_c = d * r.conv[rows, :]
            r.dproj[rows, CH : 2 * CH] = d_c.astype(bf16)
            for j in range(3):
                small[2 + j : 3 + j, :] += jnp.sum(
                    d_conv * r.mpad[s, i + 6 + j : i + 70 + j, :], axis=0, keepdims=True
                )
        r.ds[s] = r.dpad[s, 0:8, :]
        send((BACK, s), BACK, r.ds.at[s], r.dr.at[s], PREV)

    def mixer(s):
        arrived((BACK, s), r.dr.at[s])
        r.dpad[s, SEQ : SEQ + 8, :] = jnp.where(ctx < 15, r.dr[s], 0.0)
        for i in range(0, SEQ, 64):
            rows = pl.ds(s * SEQ + i, 64)
            d_mixed = (
                taps[2:3, :] * r.dpad[s, i : i + 64, :]
                + taps[1:2, :] * r.dpad[s, i + 1 : i + 65, :]
                + taps[0:1, :] * r.dpad[s, i + 2 : i + 66, :]
            )
            b, c, xi = r.proj[0, rows, :], r.proj[1, rows, :], r.proj[2, rows, :]
            d_b, d_x = (d_mixed * xi).astype(bf16), (d_mixed * b).astype(bf16)
            r.dproj[rows, 0:CH] = d_b
            r.dproj[rows, 2 * CH :] = d_x
            d_c = r.dproj[rows, CH : 2 * CH].astype(f32)
            both = d_b.astype(f32) * b + d_x.astype(f32) * xi + d_c * c
            r.lanes[i : i + 64, :] = both[:, 0:128] + both[:, 128:256]

        def term(n):
            total = nt(r.dproj[rows_of(s), 0:CH], r.wi[0, part(n), :])
            for k in (1, 2):
                total += nt(r.dproj[rows_of(s), k * CH : (k + 1) * CH], r.wi[k, part(n), :])
            return total

        sum_start(3, s, term)
        totals_start(1, s, r.lanes[...])

    back(0)
    gather_relay(B, 1)
    grad_product(DOWN, r.cg, r.hid)
    grad_first(UP)
    mixer(0)
    sum_relay(2, 0)
    back(1)
    grad_product(OUT, r.bg, r.gated)
    sum_relay(3, 0)
    grad_second(GATE)
    grad_first(DOWN)
    mixer(1)
    grad_product(IN, r.n1, r.dproj)
    deliver(1)
    sum_relay(3, 1)
    grad_second(UP)
    grad_first(OUT)

    def finish(s):
        sum_finish(3, s)
        totals_finish(1, s)

        def body(i, rows):
            g = summed(3, s, i, 32)
            value, scale = r.xg[rows, part(t)].astype(f32), r.r1[rows, :]
            small[0:1, :] += jnp.sum(g * (value * scale), axis=0, keepdims=True)
            input_grad[rows, :] = (
                r.dres[rows, :]
                + scale * (mg[...] * g)
                - value * (scale * scale * r.col[1, rows, :] * (1.0 / WIDE))
            )

        in_rows(s, 32, body)

    finish(0)
    grad_first(IN)
    grad_second(DOWN)
    sum_relay(2, 1)
    grad_last(GATE)
    finish(1)
    for n, where in enumerate((CORE, Z1, Z2, Z3, Z1C, Z2C, Z3C)):
        send((SMALL, 0), SMALL, r.sums.at[0], r.sumr.at[n], where)
    grad_second(OUT)
    grad_last(UP)
    for s in range(2):
        sum_finish(2, s)

        def body(i, rows):
            block_out[rows, :] = (r.resid[rows, :] + summed(2, s, i, 32)).astype(bf16)

        in_rows(s, 32, body)
    total = r.sums[0]
    arrived((SMALL, 0), r.sumr.at[pl.ds(0, 7)])
    for n in range(7):
        total = total + r.sumr[n]
    r.sums[1] = total
    for n, where in enumerate((X1, X2, X3)):
        send((SMALL, 1), SMALL, r.sums.at[1], r.sumr.at[7 + n], where)
    grad_second(IN)
    grad_last(DOWN)
    grad_last(OUT)
    arrived((SMALL, 1), r.sumr.at[pl.ds(7, 3)])
    for n in range(7, 10):
        total = total + r.sumr[n]
    g_small[...] = total
    grad_last(IN)

    assert len(came_ids) <= rsem.shape[0] and len(sent_ids) <= ssem.shape[0]
    for ph in range(4):
        left_all((SUM, ph), r.ys.at[ph])
    for name in gathered:
        left_all((GATHER, name), r.ys.at[0])
    left_all(TOTAL, r.rsr)
    left_all(GAINS, r.rsr.at[0, 0])
    left_all(SMALL, r.sumr)
    left_all(EDGE, r.hr)
    left_all(BACK, r.dr)
    for w in (IN, OUT, GATE, UP, DOWN):
        left_all((AHEAD, w), piece(w, 0, 0, weights[w][2]))
        left_all((GRAD, w, 0), r.paired[w])
        left_all((GRAD, w, 1), r.came[w])


def deliver_kernel(*refs):
    small, whole = refs[0], refs[1:8]
    ends, sums = refs[8:15], refs[15:18]
    held, sem = refs[18:25], refs[25]
    taken = [pltpu.make_async_copy(a, b, sem.at[0, n]) for n, (a, b) in enumerate(zip(whole, held))]
    copies = [pltpu.make_async_copy(a, b, sem.at[1, n]) for n, (a, b) in enumerate(zip(held, ends))]
    for copy in taken:
        copy.start()
    for first, then in zip(taken, copies):
        first.wait()
        then.start()
    sums[0][...] = small[0]
    sums[1][...] = small[1]
    sums[2][...] = small[2:5]
    for copy in copies:
        copy.wait()


def on_device(block_input, in_proj, out_proj, gate_proj, up_proj, down_proj, mixer_gain, ffn_gain, conv_kernel, cotangent):
    shapes = scratch()

    def kernel(*refs):
        taken, held = refs[18:], {}
        count = 0
        for name, shape in shapes.items():
            if isinstance(shape, list):
                held[name] = taken[count : count + len(shape)]
                count += len(shape)
            else:
                held[name] = taken[count]
                count += 1
        block_kernel(types.SimpleNamespace(**held), *refs[:18])

    hbm, vmem = pl.BlockSpec(memory_space=pl.ANY), pl.BlockSpec(memory_space=pltpu.VMEM)
    out = jax.ShapeDtypeStruct
    *whole, small = pl.pallas_call(
        kernel,
        out_shape=(
            out((TOK, CH), bf16),
            out((TOK, CH), f32),
            out((3, 32, CH), f32),
            out((32, CH), f32),
            out((32, HID), f32),
            out((32, HID), f32),
            out((32, HID), f32),
            out((8, CH), f32),
        ),
        in_specs=[hbm] * 7 + [vmem] * 3,
        out_specs=[vmem] * 8,
        scratch_shapes=jax.tree.leaves(list(shapes.values())),
        compiler_params=pltpu.CompilerParams(
            collective_id=0, has_side_effects=True, vmem_limit_bytes=62 * 1024 * 1024
        ),
    )(
        block_input.reshape(TOK, CH),
        cotangent.reshape(TOK, CH),
        jnp.transpose(in_proj, (1, 0, 2)),
        out_proj,
        gate_proj,
        up_proj,
        down_proj,
        mixer_gain.reshape(1, CH),
        ffn_gain.reshape(1, CH),
        conv_kernel,
    )
    block_out, input_grad, g_in, g_out, g_gate, g_up, g_down, mixer_sum, ffn_sum, taps_sum = pl.pallas_call(
        deliver_kernel,
        out_shape=(
            *(out(a.shape, a.dtype) for a in whole),
            out((CH,), f32),
            out((CH,), f32),
            out((3, CH), f32),
        ),
        in_specs=[vmem] + [hbm] * 7,
        out_specs=[hbm] * 7 + [vmem] * 3,
        scratch_shapes=[pltpu.VMEM(a.shape, a.dtype) for a in whole] + [pltpu.SemaphoreType.DMA((2, 7))],
    )(small, *whole)
    return (
        block_out.reshape(2, SEQ, CH),
        input_grad.reshape(2, SEQ, CH),
        jnp.transpose(g_in, (1, 0, 2)),
        g_out.T,
        g_gate,
        g_up,
        g_down.T,
        mixer_sum,
        ffn_sum,
        taps_sum,
    )


def solution(mesh):
    return jax.shard_map(
        on_device,
        mesh=mesh,
        in_specs=(
            P("shard", "ctx", "tp"),
            P("shard", None, "tp"),
            P("tp", "shard"),
            P("shard", "tp"),
            P("shard", "tp"),
            P("tp", "shard"),
            P("tp"),
            P("tp"),
            P(None, "tp"),
            P("shard", "ctx", "tp"),
        ),
        out_specs=(
            P("shard", "ctx", "tp"),
            P("shard", "ctx", "tp"),
            P(("shard", "ctx"), None, "tp"),
            P("tp", ("shard", "ctx")),
            P(("shard", "ctx"), "tp"),
            P(("shard", "ctx"), "tp"),
            P("tp", ("shard", "ctx")),
            P("tp"),
            P("tp"),
            P(None, "tp"),
        ),
        check_vma=False,
    )
```
